32 devices in a mesh: seq: 8 (over z, y), tp: 4 (over x, core).
Axes of the slice: x: 2, y: 2, z: 4, core: 2. Of those that a mesh axis runs over, the one named last changes fastest.
Arguments:
- stream_in: bfloat16 [2, 1536, 2048], P(None, 'seq'), may hold values from -6 to 6
- cache_keys: bfloat16 [2, 1536, 2048], P(None, 'seq', 'tp'), may hold values from -6 to 6
- cache_values: bfloat16 [2, 1536, 2048], P(None, 'seq', 'tp'), may hold values from -6 to 6
- memory: bfloat16 [2, 1536, 4096], P(None, 'seq', 'tp'), may hold values from -6 to 6
- cotangent: bfloat16 [2, 1536, 2048], P(None, 'seq'), may hold values from -6 to 6
- query_proj: bfloat16 [2048, 2048], P('seq', 'tp'), may hold values from -0.125 to 0.125
- output_proj: bfloat16 [2048, 2048], P('seq', 'tp'), may hold values from -3 to 3
- gate_first: bfloat16 [2048, 8192], P('seq', 'tp'), may hold values from -0.125 to 0.125
- up_first: bfloat16 [2048, 8192], P('seq', 'tp'), may hold values from -0.125 to 0.125
- down_first: bfloat16 [2048, 8192], P('seq', 'tp'), may hold values from -0.0625 to 0.0625
- memory_in: bfloat16 [2048, 4096], P('seq', 'tp'), may hold values from -0.125 to 0.125
- memory_out: bfloat16 [2048, 4096], P('seq', 'tp'), may hold values from -0.09375 to 0.09375
- gate_second: bfloat16 [2048, 8192], P('seq', 'tp'), may hold values from -0.125 to 0.125
- up_second: bfloat16 [2048, 8192], P('seq', 'tp'), may hold values from -0.125 to 0.125
- down_second: bfloat16 [2048, 8192], P('seq', 'tp'), may hold values from -0.0625 to 0.0625
- norm_gains: float32 [4, 2048], replicated, may hold values from 0.5 to 1.5
- group_order: int32 [16], replicated, may hold values from 0 to 15, each once
- seq_lengths: int32 [2], replicated, may hold values from 384 to 1536, as said below
Outputs:
- stream_out: bfloat16 [2, 1536, 2048], P(None, 'seq')
- stream_grad: float32 [2, 1536, 2048], P(None, 'seq')
- keys_grad: float32 [2, 1536, 2048], P(None, 'seq', 'tp')
- values_grad: float32 [2, 1536, 2048], P(None, 'seq', 'tp')
- memory_grad: float32 [2, 1536, 4096], P(None, 'seq', 'tp')
- query_grad: float32 [2048, 2048], P('seq', 'tp')
- output_grad: float32 [2048, 2048], P('seq', 'tp')
- gate_first_grad: float32 [2048, 8192], P('seq', 'tp')
- up_first_grad: float32 [2048, 8192], P('seq', 'tp')
- down_first_grad: float32 [2048, 8192], P('seq', 'tp')
- memory_in_grad: float32 [2048, 4096], P('seq', 'tp')
- memory_out_grad: float32 [2048, 4096], P('seq', 'tp')
- gate_second_grad: float32 [2048, 8192], P('seq', 'tp')
- up_second_grad: float32 [2048, 8192], P('seq', 'tp')
- down_second_grad: float32 [2048, 8192], P('seq', 'tp')
- gains_grad: float32 [4, 2048], P(None, 'seq')
The draws below stay inside these ranges and needn't reach their ends.
Inputs may be any that keep to these rules, and one draw needn't show every extreme that they name: `group_order`: each of the 16 group numbers appears once. A micro-batch's sequence fills its first seq_lengths token positions; later positions are padding whose keys no query sees. Exactly one micro-batch is full.
All inputs are finite; a program needn't handle non-finite values.
Results may differ from the reference program's by a relative error of at most 0.028.
Values may be sent and summed in bfloat16 or wider, within the bound.
No kernel may reach another device: no remote copies, remote signals or barrier semaphores. Data moves between devices by JAX's collectives and lax.ppermute only.
A program may use at most 256 MiB of HBM per device.

```python
import math
import jax
import jax.numpy as jnp
from jax import lax

D = 2048
H = 16
HD = 128
FF = 8192
DM = 4096
MB = 2
TOKENS = 1536
GROUPS = 16


def draw_seq_lengths(key, part):
    first_key = jax.random.fold_in(key, 11)
    second_key = jax.random.fold_in(key, 12)
    drawn_lengths = jax.random.randint(first_key, (MB,), TOKENS // 4, TOKENS)
    fullest = jax.random.randint(second_key, (), 0, MB)
    return jnp.where(jnp.arange(MB) == fullest, TOKENS, drawn_lengths).astype(jnp.int32)


def block_scale(key, extent, pieces, low, high):
    factor_of = 1.0
    for axis_at, parts in pieces:
        draws = jax.random.uniform(jax.random.fold_in(jax.random.fold_in(key, 6), axis_at), (parts,), jnp.float32, low / len(pieces), high / len(pieces))
        factor_of = factor_of * jnp.repeat(jnp.exp(draws), extent[axis_at] // parts).reshape((-1,) + (1,) * (len(extent) - 1 - axis_at))
    return factor_of


def scatter_about(own_key, shape, spread, limit, cuts=(), held_as=jnp.bfloat16):
    loudness = block_scale(own_key, shape, cuts, -0.22, 0.18) if cuts else 1.0
    entries = jax.random.normal(own_key, shape, jnp.float32) * spread * loudness
    return jnp.minimum(jnp.maximum(entries, -limit), limit).astype(held_as)


def setup_inputs(seed: int = 0) -> dict:
    keys = jax.random.split(jax.random.key(seed), 19)
    stream_in = scatter_about(keys[0], (MB, TOKENS, D), 1.0, 6.0, ((1, 8),))
    cache_keys = scatter_about(keys[1], (MB, TOKENS, H * HD), 1.0, 6.0, ((1, 8), (2, 4)))
    cache_values = scatter_about(keys[2], (MB, TOKENS, H * HD), 1.0, 6.0, ((1, 8), (2, 4)))
    memory = scatter_about(keys[3], (MB, TOKENS, DM), 1.0, 6.0, ((1, 8), (2, 4)))
    cotangent = scatter_about(keys[4], (MB, TOKENS, D), 1.0, 6.0, ((1, 8),))
    query_proj = scatter_about(keys[5], (D, H * HD), D ** -0.5, 0.125, ((0, 8), (1, 4)))
    output_proj = scatter_about(keys[6], (D, H * HD), 4 ** -0.5, 3.0, ((0, 8), (1, 4)))
    gate_first = scatter_about(keys[7], (D, FF), D ** -0.5, 0.125, ((0, 8), (1, 4)))
    up_first = scatter_about(keys[8], (D, FF), D ** -0.5, 0.125, ((0, 8), (1, 4)))
    down_first = scatter_about(keys[9], (D, FF), FF ** -0.5, 0.0625, ((0, 8), (1, 4)))
    memory_in = scatter_about(keys[10], (D, DM), D ** -0.5, 0.125, ((0, 8), (1, 4)))
    memory_out = scatter_about(keys[11], (D, DM), DM ** -0.5, 0.09375, ((0, 8), (1, 4)))
    gate_second = scatter_about(keys[12], (D, FF), D ** -0.5, 0.125, ((0, 8), (1, 4)))
    up_second = scatter_about(keys[13], (D, FF), D ** -0.5, 0.125, ((0, 8), (1, 4)))
    down_second = scatter_about(keys[14], (D, FF), FF ** -0.5, 0.0625, ((0, 8), (1, 4)))
    norm_gains = jnp.clip(1.0 + 0.1 * jax.random.normal(keys[15], (4, D), jnp.float32), 0.5, 1.5)
    group_order = jax.random.permutation(keys[16], GROUPS).astype(jnp.int32)
    seq_lengths = draw_seq_lengths(jax.random.fold_in(keys[18], 71), 0)
    return {"stream_in": stream_in, "cache_keys": cache_keys, "cache_values": cache_values, "memory": memory, "cotangent": cotangent, "query_proj": query_proj, "output_proj": output_proj, "gate_first": gate_first, "up_first": up_first, "down_first": down_first, "memory_in": memory_in, "memory_out": memory_out, "gate_second": gate_second, "up_second": up_second, "down_second": down_second, "norm_gains": norm_gains, "group_order": group_order, "seq_lengths": seq_lengths}


epsilon = 1e-05
masked_fill = -1e+30

@jax.custom_vjp
def low(v):
    return lax.optimization_barrier(v.astype(jnp.bfloat16)).astype(jnp.float32)

@jax.custom_vjp
def low_back(v):
    return v

def low_keep(v):
    return (low(v), None)

def low_pass(kept, grad):
    return (grad,)

def back_keep(v):
    return (v, None)

def back_low(kept, grad):
    return (low(grad),)
low.defvjp(low_keep, low_pass)
low_back.defvjp(back_keep, back_low)

def product(operand, weight):
    return jnp.matmul(operand, weight, precision=lax.Precision.HIGHEST)

def rms_apply(values_in, gain_row):
    return values_in * lax.rsqrt(lax.optimization_barrier(jnp.mean(values_in * values_in, axis=-1, keepdims=True)) + epsilon) * gain_row

def swiglu(normed, gate_weight, up_weight, down_weight):
    gate_pre = low_back(product(normed, gate_weight))
    up_pre = low_back(product(normed, up_weight))
    hidden = low(jax.nn.silu(gate_pre) * up_pre)
    return low_back(product(hidden, down_weight.T))

def attend_block(key_all, value_all, key_pos, length, query_rows, query_pos):
    scaling = HD ** (-0.5)
    scores = low_back(scaling * jnp.einsum('qhd,khd->hqk', query_rows, key_all, precision=lax.Precision.HIGHEST))
    allowed = (key_pos[None, None, :] <= query_pos[None, :, None]) & (key_pos[None, None, :] < length)
    scores = jnp.where(allowed, scores, masked_fill)
    shifted = jnp.exp(scores - lax.optimization_barrier(jnp.max(scores, axis=-1, keepdims=True)))
    probs = low(shifted / lax.optimization_barrier(jnp.sum(shifted, axis=-1, keepdims=True)))
    return jnp.einsum('hqk,khd->qhd', probs, value_all, precision=lax.Precision.HIGHEST)

def attend(queries, cache_keys, cache_values, positions, lengths):
    block_rows = math.gcd(TOKENS, 512)
    block_count = TOKENS // block_rows
    checked = jax.checkpoint(attend_block)
    outputs = []
    for batch_index in range(MB):
        query_blocks = queries[batch_index].reshape(block_count, block_rows, H, HD)
        pos_blocks = positions.reshape(block_count, block_rows)
        key_all = cache_keys[batch_index].reshape(TOKENS, H, HD)
        value_all = cache_values[batch_index].reshape(TOKENS, H, HD)
        length = lengths[batch_index]

        def one_block(paired):
            return checked(key_all, value_all, positions, length, paired[0], paired[1])
        mapped = lax.map(one_block, (query_blocks, pos_blocks))
        outputs.append(mapped.reshape(TOKENS, H * HD))
    return jnp.stack(outputs)

def forward(stream_in, cache_keys, cache_values, memory, query_proj, output_proj, gate_first, up_first, down_first, memory_in, memory_out, gate_second, up_second, down_second, norm_gains, positions, lengths):
    normed = low(rms_apply(stream_in, norm_gains[0]))
    queries = low(low_back(product(normed, query_proj)))
    attended = low(low_back(attend(queries, cache_keys, cache_values, positions, lengths)))
    stream = stream_in + low_back(product(attended, output_proj.T))
    stream = stream + swiglu(low(rms_apply(stream, norm_gains[1])), gate_first, up_first, down_first)
    normed = low(rms_apply(stream, norm_gains[2]))
    drive = low_back(product(normed, memory_in))
    gated = low(memory * jax.nn.silu(drive))
    stream = stream + low_back(product(gated, memory_out.T))
    return stream + swiglu(low(rms_apply(stream, norm_gains[3])), gate_second, up_second, down_second)

def reference(stream_in, cache_keys, cache_values, memory, cotangent, query_proj, output_proj, gate_first, up_first, down_first, memory_in, memory_out, gate_second, up_second, down_second, norm_gains, group_order, seq_lengths):
    group_len = TOKENS // GROUPS
    row_ids = jnp.arange(TOKENS, dtype=jnp.int32)
    positions = (group_order[row_ids // group_len] * group_len + row_ids % group_len).astype(jnp.int32)
    floats = tuple((item.astype(jnp.float32) for item in (stream_in, cache_keys, cache_values, memory, query_proj, output_proj, gate_first, up_first, down_first, memory_in, memory_out, gate_second, up_second, down_second, norm_gains)))

    def wrapped(*items):
        return forward(*items, positions, seq_lengths)
    result, pullback = jax.vjp(wrapped, *floats)
    grads = pullback(cotangent.astype(jnp.float32))
    return (result.astype(jnp.bfloat16), grads[0], grads[1], grads[2], grads[3], grads[4], grads[5], grads[6], grads[7], grads[8], grads[9], grads[10], grads[11], grads[12], grads[13], grads[14])
```

```python
import jax
import jax.numpy as jnp
from jax import lax
from jax.sharding import Mesh
from jax.sharding import PartitionSpec as P

HD = 128
EPS = 1e-05
FILL = -1e30
BF = jnp.bfloat16
F32 = jnp.float32
SEQ = ("ze", "zh", "zl", "y")
TP = ("x", "c")


def swap(value, axis):
    return lax.ppermute(value, axis, [(0, 1), (1, 0)])


def dot(a, b):
    return jnp.dot(a, b, preferred_element_type=F32)


def dot_nt(a, b):
    return lax.dot_general(a, b, (((1,), (1,)), ((), ())), preferred_element_type=F32)


def dot_tn(a, b):
    return lax.dot_general(a, b, (((0,), (0,)), ((), ())), preferred_element_type=F32)


def in_order(bit, own, other, axis):
    return jnp.where(
        bit == 0,
        jnp.concatenate([own, other], axis),
        jnp.concatenate([other, own], axis),
    )


def half(value, bit, axis):
    size = value.shape[axis] // 2
    return lax.dynamic_slice_in_dim(value, bit * size, size, axis)


def over_ze(value):
    if lax.axis_size("ze") == 1:
        return value
    return lax.all_gather(value, "ze", axis=0, tiled=True)


def total_ze(value):
    if lax.axis_size("ze") == 1:
        return value
    return lax.psum_scatter(value.astype(BF), "ze", scatter_dimension=0, tiled=True).astype(F32)


class Place:
    def __init__(self, width):
        self.zh = lax.axis_index("zh")
        self.zl = lax.axis_index("zl")
        self.y = lax.axis_index("y")
        self.x = lax.axis_index("x")
        self.c = lax.axis_index("c")
        self.ze = lax.axis_size("ze")
        self.rows = width // (self.ze * 8)

    def turn(self, value):
        lead = value.shape[:-1]
        n = len(lead)
        v = value.reshape(lead + (self.ze, 2, 2, 2, self.rows))
        v = jnp.moveaxis(v, n + 3, n)
        v = jnp.where(self.y == 1, jnp.flip(v, n), v)
        v = jnp.where(self.zh == 1, jnp.flip(v, n + 2), v)
        return v.reshape(value.shape)

    def turn_back(self, value):
        lead = value.shape[:-1]
        n = len(lead)
        v = value.reshape(lead + (2, self.ze, 2, 2, self.rows))
        v = jnp.where(self.y == 1, jnp.flip(v, n), v)
        v = jnp.where(self.zh == 1, jnp.flip(v, n + 2), v)
        v = jnp.moveaxis(v, n, n + 3)
        return v.reshape(value.shape)

    def gather(self, w):
        a = in_order(self.zl, half(w, self.zl, 1), swap(half(w, 1 - self.zl, 1), "zl"), 0)
        b = jnp.concatenate([a, swap(a, "zh")], 0)
        b = over_ze(b)
        p = swap(b, "y")
        return jnp.concatenate(
            [
                jnp.concatenate([b, swap(b, "c")], 1),
                jnp.concatenate([p, swap(p, "c")], 1),
            ],
            0,
        )

    def scatter(self, left, right):
        d = left.shape[1] // 2
        k = right.shape[1] // 2
        l_own, l_far = left[:, :d], left[:, d:]
        r_own, r_far = right[:, :k], right[:, k:]
        got_far = swap(dot_tn(l_far, r_far).astype(BF), "c")
        got_own = swap(dot_tn(l_own, r_far).astype(BF), "c")
        t_far = (dot_tn(l_far, r_own) + got_far.astype(F32)).astype(BF)
        got_y = swap(t_far, "y")
        t = (dot_tn(l_own, r_own) + got_own.astype(F32) + got_y.astype(F32)).astype(BF)
        t = total_ze(t)
        m = t.shape[0] // 2
        u = (t[:m].astype(F32) + swap(t[m:].astype(BF), "zh").astype(F32)).astype(BF)
        own = half(u, self.zl, 0)
        got = swap(half(u, 1 - self.zl, 0), "zl")
        return in_order(self.zl, own, got, 1).astype(F32)

    def gather_rows(self, w):
        a = in_order(self.zl, w, swap(w, "zl"), 0)
        b = jnp.concatenate([a, swap(a, "zh")], 0)
        b = over_ze(b)
        return jnp.concatenate([b, swap(b, "y")], 0)

    def scatter_rows(self, left, right):
        d = left.shape[1] // 2
        got = swap(dot_tn(left[:, d:], right).astype(BF), "y")
        t = (dot_tn(left[:, :d], right) + got.astype(F32)).astype(BF)
        t = total_ze(t)
        m = t.shape[0] // 2
        u = t[:m].astype(F32) + swap(t[m:].astype(BF), "zh").astype(F32)
        own = half(u, self.zl, 0)
        return own + swap(half(u, 1 - self.zl, 0).astype(BF), "zl").astype(F32)

    def spread(self, v):
        h = v.shape[1] // 2
        vx = swap(v, "x")
        vz = swap(v, "zl")
        both = jnp.concatenate([swap(vz[:, :h], "x"), swap(vx[:, h:], "zl")], 1)
        return jnp.concatenate([v, vx, vz, both], 0)

    def collect(self, part):
        t, d = part.shape
        h = d // 2
        part = part.reshape(4, t // 4, d)
        a, b = part[..., :h], part[..., h:]
        got_a = swap(a[2:].astype(BF), "zl").astype(F32)
        got_b = swap(b[1::2].astype(BF), "x").astype(F32)
        a_x = (a[1] + got_a[1]).astype(BF)
        b_z = (b[2] + got_b[1]).astype(BF)
        a0 = a[0] + got_a[0] + swap(a_x, "x").astype(F32)
        b0 = b[0] + got_b[0] + swap(b_z, "zl").astype(F32)
        return jnp.concatenate([a0, b0], 1)

    def own_rows(self, v):
        mb, t, d = v.shape
        v = v.reshape(mb, 4, t // 4, d)
        v = lax.dynamic_slice_in_dim(v, self.x * 2 + self.c, 1, 1)
        return v.reshape(mb * t // 4, d)

    def spread_tp(self, v, mb):
        vc = swap(v, "c")
        pair = in_order(
            self.c, v.reshape(mb, 1, -1, v.shape[1]), vc.reshape(mb, 1, -1, v.shape[1]), 1
        )
        far = swap(pair, "x")
        full = in_order(self.x, pair, far, 1)
        return full.reshape(mb, -1, v.shape[1])

    def collect_tp(self, part, mb):
        t, d = part.shape
        part = part.reshape(mb, 2, 2, t // (4 * mb), d)
        mine = half(part, self.c, 2)
        mine = mine + swap(half(part, 1 - self.c, 2).astype(BF), "c").astype(F32)
        own = half(mine, self.x, 1)
        own = own + swap(half(mine, 1 - self.x, 1).astype(BF), "x").astype(F32)
        return own.reshape(t // 4, d)

    def memory_in(self, m):
        mb, t, k = m.shape
        v = m.reshape(mb, 2, 2, t // 4, 2, k // 2)
        keep = half(v, self.c, 2)
        got = swap(half(v, 1 - self.c, 2), "c")
        w = jnp.concatenate([keep, got], 2)
        keep = half(w, self.zl, 4)
        got = swap(half(w, 1 - self.zl, 4), "zl")
        out = jnp.concatenate([keep, got], 4)
        out = jnp.where(self.x == 1, jnp.flip(out, 1), out)
        return out.transpose(4, 1, 0, 3, 2, 5).reshape(4 * mb * t // 4, k)

    def memory_out(self, g, mb):
        t, k = g.shape
        v = g.reshape(2, 2, mb, t // (4 * mb), 2, k // 2).transpose(2, 1, 4, 3, 0, 5)
        v = jnp.where(self.x == 1, jnp.flip(v, 1), v)
        own, far = v[..., 0, :], v[..., 1, :]
        got = swap(far.astype(BF), "zl").astype(F32)
        w = in_order(self.zl, own[..., None, :], got[..., None, :], 4)
        own, far = w[:, :, 0], w[:, :, 1]
        got = swap(far.astype(BF), "c").astype(F32)
        full = in_order(self.c, own[:, :, None], got[:, :, None], 2)
        return full.reshape(mb, t // mb, k)


def rms(v, g):
    r = lax.rsqrt(jnp.mean(v * v, axis=-1, keepdims=True) + EPS)
    return v * r * g


def rms_back(v, g, dn):
    r = lax.rsqrt(jnp.mean(v * v, axis=-1, keepdims=True) + EPS)
    gain = jnp.sum(dn * v * r, axis=0)
    gd = g * dn
    return r * gd - v * (r * r * r) * jnp.mean(v * gd, axis=-1, keepdims=True), gain


def silu_parts(v):
    s = jax.nn.sigmoid(v)
    return v * s, s * (1.0 + v * (1.0 - s))


def to_pairs(v):
    mb, t, k = v.shape
    v = v.reshape(mb, t, k // HD, HD).transpose(0, 2, 1, 3).reshape(-1, t, HD)
    v = lax.all_to_all(v, ("zh", "zl", "y"), split_axis=0, concat_axis=0, tiled=True)
    return v.reshape(-1, HD)


def from_pairs(v, mb, t):
    v = v.reshape(8, t, HD)
    v = lax.all_to_all(v, ("zh", "zl", "y"), split_axis=0, concat_axis=0, tiled=True)
    return v.reshape(mb, -1, t, HD).transpose(0, 2, 1, 3).reshape(mb, t, -1)


def positions(order, first, count, group_len):
    ids = first + jnp.arange(count, dtype=jnp.int32)
    slots = jnp.arange(order.shape[0], dtype=jnp.int32)
    group = jnp.sum(
        jnp.where((ids // group_len)[:, None] == slots[None, :], order[None, :], 0), axis=1
    )
    return group * group_len + ids % group_len


def shards(
    stream_in,
    cache_keys,
    cache_values,
    memory,
    cotangent,
    query_proj,
    output_proj,
    gate_first,
    up_first,
    down_first,
    memory_in,
    memory_out,
    gate_second,
    up_second,
    down_second,
    norm_gains,
    group_order,
    seq_lengths,
):
    mb, tok, width = stream_in.shape
    at = Place(width)
    scaling = HD ** (-0.5)
    groups = group_order.shape[0]
    tokens = tok * at.ze * 8
    group_len = tokens // groups

    gains = at.turn(norm_gains)
    stream = at.turn(stream_in)
    cot = at.turn(cotangent)
    r0 = at.own_rows(stream).astype(F32)

    wq = at.gather_rows(query_proj)
    wo = at.gather_rows(output_proj)
    keys = over_ze(to_pairs(cache_keys))
    values = over_ze(to_pairs(cache_values))

    n1 = rms(stream.astype(F32).reshape(mb * tok, width), gains[0]).astype(BF)
    q = to_pairs(dot(n1, wq).astype(BF).reshape(mb, tok, -1))

    g1, u1, d1 = at.gather(gate_first), at.gather(up_first), at.gather(down_first)
    mi, mo = at.gather(memory_in), at.gather(memory_out)
    g2, u2, d2 = at.gather(gate_second), at.gather(up_second), at.gather(down_second)

    pair = (at.zh * 2 + at.zl) * 2 + at.y
    heads = cache_keys.shape[2] // HD
    batch = pair // heads
    length = lax.dynamic_slice_in_dim(seq_lengths, batch, 1, 0)
    q_rows = q.shape[0]
    k_rows = keys.shape[0]
    q_pos = positions(group_order, lax.axis_index("ze") * q_rows, q_rows, group_len)
    k_pos = positions(group_order, 0, k_rows, group_len)
    allowed = (k_pos[None, :] <= q_pos[:, None]) & (k_pos < length)[None, :]
    s = jnp.where(allowed, dot_nt(q, keys) * scaling, FILL)
    top = jnp.max(s, axis=1, keepdims=True)
    e = jnp.exp(s - top)
    total = jnp.sum(e, axis=1, keepdims=True)
    o = dot(e.astype(BF), values) / total
    lse = top + jnp.log(total)
    attn = from_pairs(o.astype(BF), mb, tok).reshape(mb * tok, -1)

    x1 = r0 + at.collect_tp(dot_nt(attn, wo), mb)

    n2 = at.spread(rms(x1, gains[1]).astype(BF))
    ga, ua = dot(n2, g1), dot(n2, u1)
    ha = (jax.nn.silu(ga) * ua).astype(BF)
    x2 = x1 + at.collect(dot_nt(ha, d1))

    mem = at.memory_in(memory).astype(F32)
    n3 = at.spread(rms(x2, gains[2]).astype(BF))
    za = dot(n3, mi)
    gm = (mem * jax.nn.silu(za)).astype(BF)
    x3 = x2 + at.collect(dot_nt(gm, mo))

    n4 = at.spread(rms(x3, gains[3]).astype(BF))
    gb, ub = dot(n4, g2), dot(n4, u2)
    hb = (jax.nn.silu(gb) * ub).astype(BF)
    x4 = x3 + at.collect(dot_nt(hb, d2))
    stream_out = at.spread_tp(at.turn_back(x4.astype(BF)), mb)

    cv = cot.reshape(mb, 2, 2, tok // 4, width)
    cv = half(cv, at.c, 2)
    cv = jnp.where(at.x == 1, jnp.flip(cv, 1), cv)
    cv = cv.transpose(1, 2, 0, 3, 4).reshape(mb * tok // 2, width)
    yb = jnp.concatenate([cv, swap(cv, "zl")], 0)

    def ffn_back(y, n, gate, up, hidden, wg, wu, wd):
        dh = dot(y, wd)
        act, slope = silu_parts(gate)
        dg = (dh * up * slope).astype(BF)
        du = (dh * act).astype(BF)
        dn = at.collect(dot_nt(dg, wg) + dot_nt(du, wu))
        return dn, at.scatter(n, dg), at.scatter(n, du), at.scatter(y, hidden)

    dn4, gate_second_grad, up_second_grad, down_second_grad = ffn_back(
        yb, n4, gb, ub, hb, g2, u2, d2
    )
    back, gain4 = rms_back(x3, gains[3], dn4)
    dx3 = at.own_rows(cot).astype(F32) + back

    yg = at.spread(dx3.astype(BF))
    dgm = dot(yg, mo)
    act, slope = silu_parts(za)
    memory_grad = at.memory_out(dgm * act, mb)
    dza = (dgm * mem * slope).astype(BF)
    dn3 = at.collect(dot_nt(dza, mi))
    memory_in_grad = at.scatter(n3, dza)
    memory_out_grad = at.scatter(yg, gm)
    back, gain3 = rms_back(x2, gains[2], dn3)
    dx2 = dx3 + back

    ya = at.spread(dx2.astype(BF))
    dn2, gate_first_grad, up_first_grad, down_first_grad = ffn_back(
        ya, n2, ga, ua, ha, g1, u1, d1
    )
    back, gain2 = rms_back(x1, gains[1], dn2)
    dx1 = dx2 + back

    yo = at.spread_tp(dx1.astype(BF), mb).reshape(mb * tok, width)
    do = to_pairs(dot(yo, wo).astype(BF).reshape(mb, tok, -1))
    output_grad = at.scatter_rows(yo, attn)
    delta = jnp.sum(do.astype(F32) * o, axis=1, keepdims=True)
    p = jnp.exp(s - lse)
    ds = (p * (dot_nt(do, values) - delta)).astype(BF)
    dq = from_pairs((dot(ds, keys) * scaling).astype(BF), mb, tok)
    dk = total_ze(dot_tn(ds, q) * scaling).astype(BF)
    dv = total_ze(dot_tn(p.astype(BF), do)).astype(BF)
    keys_grad = from_pairs(dk, mb, tok).astype(F32)
    values_grad = from_pairs(dv, mb, tok).astype(F32)
    dq = dq.reshape(mb * tok, -1)
    dn1 = at.collect_tp(dot_nt(dq, wq), mb)
    query_grad = at.scatter_rows(n1, dq)
    back, gain1 = rms_back(r0, gains[0], dn1)
    stream_grad = at.spread_tp(at.turn_back((dx1 + back).astype(BF)), mb).astype(F32)

    gain = at.turn_back(jnp.stack([gain1, gain2, gain3, gain4]))
    for axis in ("c", "x", "y", "zh", "zl"):
        gain = gain + swap(gain, axis)
    if at.ze > 1:
        gain = lax.psum(gain, "ze")
    spot = (lax.axis_index("ze") * 2 + at.zh) * 4 + at.zl * 2 + at.y
    gains_grad = lax.dynamic_slice_in_dim(gain, spot * at.rows, at.rows, 1)

    return (
        stream_out,
        stream_grad,
        keys_grad,
        values_grad,
        memory_grad,
        query_grad,
        output_grad,
        gate_first_grad,
        up_first_grad,
        down_first_grad,
        memory_in_grad,
        memory_out_grad,
        gate_second_grad,
        up_second_grad,
        down_second_grad,
        gains_grad,
    )


def solution(mesh):
    seq, tp = mesh.shape["seq"], mesh.shape["tp"]
    fine = Mesh(
        mesh.devices.reshape(seq // 8, 2, 2, 2, tp // 2, 2), ("ze", "zh", "zl", "y", "x", "c")
    )
    tokens = P(None, SEQ, None)
    both = P(None, SEQ, TP)
    weight = P(SEQ, TP)
    return jax.shard_map(
        shards,
        mesh=fine,
        in_specs=(tokens, both, both, both, tokens) + (weight,) * 10 + (P(), P(), P()),
        out_specs=(tokens, tokens, both, both, both) + (weight,) * 10 + (P(None, SEQ),),
        check_vma=False,
    )
```

```python
import jax
import jax.numpy as jnp
from jax import lax
from jax.sharding import Mesh
from jax.sharding import PartitionSpec as P

HD = 128
EPS = 1e-05
FILL = -1e30
BF = jnp.bfloat16
F32 = jnp.float32
SEQ = ("ze", "zh", "zl", "y")
TP = ("x", "c")
GROUP = ("zh", "zl", "y")
UNIT = ("zl", "y", "x", "c")


def swap(value, axis):
    return lax.ppermute(value, axis, [(0, 1), (1, 0)])


def after(value, earlier):
    return lax.optimization_barrier((value, earlier))[0]


def dot(a, b):
    return jnp.dot(a, b, preferred_element_type=F32)


def dot_nt(a, b):
    return lax.dot_general(a, b, (((1,), (1,)), ((), ())), preferred_element_type=F32)


def dot_tn(a, b):
    return lax.dot_general(a, b, (((0,), (0,)), ((), ())), preferred_element_type=F32)


def in_order(bit, own, other, axis):
    return jnp.where(
        bit == 0,
        jnp.concatenate([own, other], axis),
        jnp.concatenate([other, own], axis),
    )


def half(value, bit, axis):
    size = value.shape[axis] // 2
    return lax.dynamic_slice_in_dim(value, bit * size, size, axis)


def trade(value, axes):
    return lax.all_to_all(value, axes, split_axis=0, concat_axis=0, tiled=True)


def copies(value, n):
    return jnp.broadcast_to(value[None], (n,) + value.shape)


def over_ze(value):
    if lax.axis_size("ze") == 1:
        return value
    return lax.all_gather(value, "ze", axis=0, tiled=True)


def total_ze(value):
    if lax.axis_size("ze") == 1:
        return value
    return lax.psum_scatter(value.astype(BF), "ze", scatter_dimension=0, tiled=True).astype(F32)


class Place:
    def __init__(self, width):
        self.zl = lax.axis_index("zl")
        self.x = lax.axis_index("x")
        self.y = lax.axis_index("y")
        self.c = lax.axis_index("c")
        self.ze = lax.axis_size("ze")
        self.rows = width // (self.ze * 8)
        self.line = []
        self.first = []

    def ordered(self, value, axes):
        if self.line:
            value = after(value, self.line[-1])
        if self.first:
            value = after(value, tuple(self.first))
            self.first = []
        self.line.append(trade(value, axes))
        return self.line[-1]

    def gather(self, w):
        r, k = w.shape
        w = w.reshape(r, 4, k // 4).transpose(1, 0, 2)
        w = self.ordered(jnp.concatenate([w, w]), GROUP)
        w = over_ze(w.reshape(8 * r, k // 4))
        own = lax.all_gather(w, "x", axis=1, tiled=True)
        return own, swap(own, "c")

    def open_grad(self, left, far):
        part = dot_tn(left, far).astype(BF)
        return part, swap(part, "c")

    def close_grad(self, left, own, got):
        part = (dot_tn(left, own) + got.astype(F32)).astype(BF)
        t = lax.psum_scatter(part, "x", scatter_dimension=1, tiled=True)
        t = total_ze(t).astype(BF).reshape(8, self.rows, -1)
        t = self.ordered(t, GROUP).astype(F32)
        t = t[:4] + t[4:]
        return part, t.transpose(1, 0, 2).reshape(self.rows, -1)

    def gather_rows(self, w):
        a = self.ordered(copies(w, 4), ("zh", "zl"))
        a = over_ze(a)
        return lax.all_gather(a, "y", axis=1, tiled=True).reshape(-1, w.shape[1])

    def scatter_rows(self, left, right):
        part = dot_tn(left, right).astype(BF)
        t = part.reshape(-1, 2 * self.rows, right.shape[1])
        t = lax.psum_scatter(t, "y", scatter_dimension=1, tiled=True)
        t = self.ordered(total_ze(t).astype(BF), ("zh", "zl")).astype(F32)
        return part, (t[0] + t[1]) + (t[2] + t[3])

    def spread(self, v):
        h = v.shape[1] // 2
        vy = swap(v, "y")
        vz = swap(v, "zl")
        both = jnp.concatenate([swap(vz[:, :h], "y"), swap(vy[:, h:], "zl")], 1)
        return jnp.concatenate([v, vy, vz, both], 0)

    def collect(self, part):
        t, d = part.shape
        h = d // 2
        part = part.reshape(4, t // 4, d)
        a, b = part[..., :h], part[..., h:]
        got_a = swap(a[2:].astype(BF), "zl").astype(F32)
        got_b = swap(b[1::2].astype(BF), "y").astype(F32)
        a_y = (a[1] + got_a[1]).astype(BF)
        b_z = (b[2] + got_b[1]).astype(BF)
        a0 = a[0] + got_a[0] + swap(a_y, "y").astype(F32)
        b0 = b[0] + got_b[0] + swap(b_z, "zl").astype(F32)
        return jnp.concatenate([a0, b0], 1)

    def own_rows(self, v):
        mb, t, d = v.shape
        v = v.reshape(mb, 4, t // 4, d)
        v = lax.dynamic_slice_in_dim(v, self.x * 2 + self.c, 1, 1)
        return v.reshape(mb * t // 4, d)

    def spread_tp(self, v, mb):
        d = v.shape[1]
        v = v.reshape(mb, 1, -1, d)
        pair = in_order(self.c, v, swap(v, "c"), 1)
        full = in_order(self.x, pair, swap(pair, "x"), 1)
        return full.reshape(mb, -1, d)

    def collect_tp(self, part, mb):
        t, d = part.shape
        part = part.reshape(mb, 2, 2, t // (4 * mb), d)
        mine = half(part, self.c, 2)
        mine = mine + swap(half(part, 1 - self.c, 2).astype(BF), "c").astype(F32)
        own = half(mine, self.x, 1)
        own = own + swap(half(mine, 1 - self.x, 1).astype(BF), "x").astype(F32)
        return own.reshape(t // 4, d)

    def flips(self, v, axis):
        v = jnp.where(self.zl == 1, jnp.flip(v, axis), v)
        return jnp.where(self.y == 1, jnp.flip(v, axis + 1), v)

    def memory_in(self, m):
        mb, t, k = m.shape
        v = m.reshape(mb, 4, t // 4, 4, k // 4).transpose(3, 1, 0, 2, 4)
        v = trade(v.reshape(16, mb * t // 4, k // 4), UNIT)
        v = self.flips(v.reshape(2, 2, 2, 2, mb * t // 4, k // 4), 0)
        v = v.transpose(3, 0, 1, 4, 2, 5).reshape(2, mb * t, k // 2)
        return jnp.where(self.c == 0, v[0], v[1]), jnp.where(self.c == 0, v[1], v[0])

    def memory_out(self, own, far, mb):
        t, k = own.shape[0], own.shape[1] * 2
        v = in_order(self.c, own.astype(BF)[None], far.astype(BF)[None], 0)
        v = v.reshape(2, 2, 2, t // 4, 2, k // 4).transpose(1, 2, 4, 0, 3, 5)
        v = self.flips(v, 0).reshape(16, t // 4, k // 4)
        v = trade(v, UNIT).reshape(4, 4, mb, t // (4 * mb), k // 4)
        return v.transpose(2, 1, 3, 0, 4).reshape(mb, t // mb, k).astype(F32)


def rms(v, g):
    r = lax.rsqrt(jnp.mean(v * v, axis=-1, keepdims=True) + EPS)
    return v * r * g


def rms_back(v, g, dn):
    r = lax.rsqrt(jnp.mean(v * v, axis=-1, keepdims=True) + EPS)
    gain = jnp.sum(dn * v * r, axis=0)
    gd = g * dn
    return r * gd - v * (r * r * r) * jnp.mean(v * gd, axis=-1, keepdims=True), gain


def silu_parts(v):
    s = jax.nn.sigmoid(v)
    return v * s, s * (1.0 + v * (1.0 - s))


def exchange(v):
    here = lax.axis_index(GROUP)
    out = []
    for k in range(8):
        block = lax.dynamic_index_in_dim(v, here ^ k, 0, keepdims=False)
        out.append(block if k == 0 else lax.ppermute(block, GROUP, [(i, i ^ k) for i in range(8)]))
    return out


def to_pairs(v):
    n, mb, t, k = v.shape
    v = v.reshape(n, mb, t, k // HD, HD).transpose(1, 3, 0, 2, 4).reshape(-1, n, t, HD)
    return jnp.concatenate(exchange(v), 1)


def from_pairs(v, mb, t):
    n = v.shape[0]
    here = lax.axis_index(GROUP)
    v = v.reshape(n, 8, t, HD)
    got = [v[:, 0]]
    for k in range(1, 8):
        got.append(lax.ppermute(v[:, k], GROUP, [(i, i ^ k) for i in range(8)]))
    v = jnp.stack(got)
    v = jnp.stack([lax.dynamic_index_in_dim(v, here ^ k, 0, keepdims=False) for k in range(8)])
    return v.reshape(mb, -1, n, t, HD).transpose(2, 0, 3, 1, 4).reshape(n, mb, t, -1)


def positions(order, ids, group_len):
    slots = jnp.arange(order.shape[0], dtype=jnp.int32)
    group = jnp.sum(
        jnp.where((ids // group_len)[:, None] == slots[None, :], order[None, :], 0), axis=1
    )
    return group * group_len + ids % group_len


def shards(
    stream_in,
    cache_keys,
    cache_values,
    memory,
    cotangent,
    query_proj,
    output_proj,
    gate_first,
    up_first,
    down_first,
    memory_in,
    memory_out,
    gate_second,
    up_second,
    down_second,
    norm_gains,
    group_order,
    seq_lengths,
):
    mb, tok, width = stream_in.shape
    at = Place(width)
    scaling = HD ** (-0.5)
    groups = group_order.shape[0]
    tokens = tok * at.ze * 8
    group_len = tokens // groups

    gains = norm_gains
    stream = stream_in
    r0 = at.own_rows(stream).astype(F32)

    wq = at.gather_rows(query_proj)
    cache = to_pairs(jnp.stack([cache_keys, cache_values], 0))
    keys, values = over_ze(cache[0]), over_ze(cache[1])
    g1 = at.gather(gate_first)
    wo = at.gather_rows(output_proj)
    at.first = [cache]
    u1 = at.gather(up_first)
    n1 = rms(stream.astype(F32).reshape(mb * tok, width), gains[0]).astype(BF)
    q = to_pairs(dot(n1, wq).astype(BF).reshape(1, mb, tok, -1))[0]
    q = after(q, wo)
    at.first = [q]
    d1 = at.gather(down_first)

    pair = lax.axis_index(("zh", "zl", "y"))
    heads = cache_keys.shape[2] // HD
    batch = pair // heads
    length = lax.dynamic_slice_in_dim(seq_lengths, batch, 1, 0)
    q_rows = q.shape[0]
    k_rows = keys.shape[0]
    rows = jnp.arange(k_rows, dtype=jnp.int32)
    ids = rows // q_rows * q_rows + (rows % q_rows // tok ^ pair) * tok + rows % tok
    k_pos = positions(group_order, ids, group_len)
    q_pos = lax.dynamic_slice_in_dim(k_pos, lax.axis_index("ze") * q_rows, q_rows, 0)
    allowed = (k_pos[None, :] <= q_pos[:, None]) & (k_pos < length)[None, :]
    s = jnp.where(allowed, dot_nt(q, keys) * scaling, FILL)
    top = jnp.max(s, axis=1, keepdims=True)
    e = jnp.exp(s - top)
    total = jnp.sum(e, axis=1, keepdims=True)
    o = dot(e.astype(BF), values) / total
    lse = top + jnp.log(total)
    attn = from_pairs(o.astype(BF)[None], mb, tok).reshape(mb * tok, -1)

    at.first = [attn]
    mi, mo = at.gather(memory_in), at.gather(memory_out)
    x1 = r0 + at.collect_tp(dot_nt(attn, wo), mb)
    at.first = [x1]
    g2 = at.gather(gate_second)

    def ffn(x, gain, wg, wu, wd, pins):
        n = after(at.spread(rms(x, gain).astype(BF)), pins)
        gate = [dot(n, w) for w in wg]
        up = [dot(n, w) for w in wu]
        hidden = [(jax.nn.silu(g) * u).astype(BF) for g, u in zip(gate, up)]
        out = at.collect(dot_nt(hidden[0], wd[0]) + dot_nt(hidden[1], wd[1]))
        return x + out, (n, gate, up, hidden)

    x2, kept1 = ffn(x1, gains[1], g1, u1, d1, ())
    at.first = [kept1[0]]
    u2 = at.gather(up_second)
    at.first = [kept1[3][1]]
    d2 = at.gather(down_second)

    mem = at.memory_in(memory)
    n3 = at.spread(rms(x2, gains[2]).astype(BF))
    za = [dot(n3, w) for w in mi]
    gm = [(m.astype(F32) * jax.nn.silu(z)).astype(BF) for m, z in zip(mem, za)]
    x3 = x2 + at.collect(dot_nt(gm[0], mo[0]) + dot_nt(gm[1], mo[1]))

    x4, kept2 = ffn(x3, gains[3], g2, u2, d2, ())
    stream_out = at.spread_tp(x4.astype(BF), mb)

    cot = at.own_rows(cotangent)
    yb = at.spread(cot)

    zline = at.line

    def ffn_back(y, kept, wg, wu, wd, pins):
        n, gate, up, hidden = kept
        far_d, got_d = at.open_grad(y, hidden[1])
        y2 = after(y, far_d)
        dg, du = [], []
        for g, u, w in zip(gate, up, wd):
            dh = dot(y2, w)
            act, slope = silu_parts(g)
            dg.append((dh * u * slope).astype(BF))
            du.append((dh * act).astype(BF))
        part_d, down_grad = at.close_grad(y, hidden[0], got_d)
        dg, du = after((dg, du), (part_d,) + pins)
        dn = dot_nt(dg[0], wg[0]) + dot_nt(dg[1], wg[1])
        dn = dn + dot_nt(du[0], wu[0]) + dot_nt(du[1], wu[1])
        far_g, got_g = at.open_grad(n, dg[1])
        far_u, got_u = at.open_grad(n, du[1])
        dn = after(at.collect(dn), (far_g, far_u))
        return dn, down_grad, (n, dg[0], got_g), (n, du[0], got_u)

    dn4, down_second_grad, open_g, open_u = ffn_back(yb, kept2, g2, u2, d2, ())
    back, gain4 = rms_back(x3, gains[3], dn4)
    dx3 = cot.astype(F32) + back

    part_g, gate_second_grad = at.close_grad(*open_g)
    yg = after(at.spread(dx3.astype(BF)), part_g)
    part_u, up_second_grad = at.close_grad(*open_u)
    far, got = at.open_grad(yg, gm[1])
    dz, dm = [], []
    for w, z, m in zip(mo, za, mem):
        dgm = dot(yg, w)
        act, slope = silu_parts(z)
        dm.append(dgm * act)
        dz.append((dgm * m.astype(F32) * slope).astype(BF))
    dz = after(dz, (part_u, far))
    dn3 = dot_nt(dz[0], mi[0]) + dot_nt(dz[1], mi[1])
    part_o, memory_out_grad = at.close_grad(yg, gm[0], got)
    far, got = at.open_grad(n3, dz[1])
    dn3 = after(at.collect(dn3), (part_o, far, zline[10]))
    memory_grad = at.memory_out(dm[0], dm[1], mb)
    back, gain3 = rms_back(x2, gains[2], dn3)
    dx2 = dx3 + back

    part_i, memory_in_grad = at.close_grad(n3, dz[0], got)
    ya = after(at.spread(dx2.astype(BF)), (part_i, zline[11]))
    dn2, down_first_grad, open_g, open_u = ffn_back(ya, kept1, g1, u1, d1, (zline[12],))
    dn2 = after(dn2, (zline[13], zline[14]))
    back, gain2 = rms_back(x1, gains[1], dn2)
    dx1 = dx2 + back

    part_g, gate_first_grad = at.close_grad(*open_g)
    yo = after(at.spread_tp(dx1.astype(BF), mb), (part_g, zline[15])).reshape(mb * tok, width)
    part_u, up_first_grad = at.close_grad(*open_u)
    do = to_pairs(dot(yo, wo).astype(BF).reshape(1, mb, tok, -1))[0]
    do = after(do, part_u)
    part_w, output_grad = at.scatter_rows(yo, attn)
    delta = jnp.sum(do.astype(F32) * o, axis=1, keepdims=True)
    p = jnp.exp(s - lse)
    ds = (p * (dot_nt(do, values) - delta)).astype(BF)
    dq = after((dot(ds, keys) * scaling).astype(BF)[None], (part_w, zline[16]))
    dq = from_pairs(dq, mb, tok)
    dk = total_ze(dot_tn(ds, q) * scaling).astype(BF)
    dv = total_ze(dot_tn(p.astype(BF), do)).astype(BF)
    dkv = from_pairs(after(jnp.stack([dk, dv]), dq), mb, tok).astype(F32)
    keys_grad, values_grad = dkv[0], dkv[1]
    dq = dq.reshape(mb * tok, -1)
    dn1 = at.collect_tp(dot_nt(dq, wq), mb)
    _, query_grad = at.scatter_rows(n1, dq)
    back, gain1 = rms_back(r0, gains[0], dn1)
    stream_grad = at.spread_tp((dx1 + back).astype(BF), mb).astype(F32)

    gain = jnp.stack([gain1, gain2, gain3, gain4])
    for axis in ("c", "x", "y", "zh", "zl"):
        gain = gain + swap(gain, axis)
    if at.ze > 1:
        gain = lax.psum(gain, "ze")
    spot = lax.axis_index(SEQ)
    gains_grad = lax.dynamic_slice_in_dim(gain, spot * at.rows, at.rows, 1)

    return (
        stream_out,
        stream_grad,
        keys_grad,
        values_grad,
        memory_grad,
        query_grad,
        output_grad,
        gate_first_grad,
        up_first_grad,
        down_first_grad,
        memory_in_grad,
        memory_out_grad,
        gate_second_grad,
        up_second_grad,
        down_second_grad,
        gains_grad,
    )


def solution(mesh):
    seq, tp = mesh.shape["seq"], mesh.shape["tp"]
    fine = Mesh(
        mesh.devices.reshape(seq // 8, 2, 2, 2, tp // 2, 2), ("ze", "zh", "zl", "y", "x", "c")
    )
    tokens = P(None, SEQ, None)
    both = P(None, SEQ, TP)
    weight = P(SEQ, TP)
    return jax.shard_map(
        shards,
        mesh=fine,
        in_specs=(tokens, both, both, both, tokens) + (weight,) * 10 + (P(), P(), P()),
        out_specs=(tokens, tokens, both, both, both) + (weight,) * 10 + (P(None, SEQ),),
        check_vma=False,
    )
```

```python
import jax
import jax.numpy as jnp
from jax import lax
from jax.experimental import pallas as pl
from jax.sharding import Mesh
from jax.sharding import PartitionSpec as P

HD = 128
EPS = 1e-05
FILL = -1e30
BF = jnp.bfloat16
F32 = jnp.float32
SEQ = ("ze", "zh", "zl", "y")
TP = ("x", "c")
GROUP = ("zh", "zl", "y")
UNIT = ("zl", "y", "x", "c")


def swap(value, axis):
    return lax.ppermute(value, axis, [(0, 1), (1, 0)])


def after(value, earlier):
    return lax.optimization_barrier((value, earlier))[0]


def held(value, *earlier):
    earlier = jax.tree.leaves(earlier)
    if not earlier:
        return value
    anywhere = pl.BlockSpec(memory_space=pl.ANY)

    def body(*refs):
        pass

    return pl.pallas_call(
        body,
        in_specs=[anywhere] * (1 + len(earlier)),
        out_specs=anywhere,
        out_shape=jax.ShapeDtypeStruct(value.shape, value.dtype),
        input_output_aliases={0: 0},
        cost_estimate=pl.CostEstimate(flops=0, bytes_accessed=0, transcendentals=0),
    )(value, *earlier)


def dot(a, b):
    return jnp.dot(a, b, preferred_element_type=F32)


def dot_nt(a, b):
    return lax.dot_general(a, b, (((1,), (1,)), ((), ())), preferred_element_type=F32)


def dot_tn(a, b):
    return lax.dot_general(a, b, (((0,), (0,)), ((), ())), preferred_element_type=F32)


def in_order(bit, own, other, axis):
    return jnp.where(
        bit == 0,
        jnp.concatenate([own, other], axis),
        jnp.concatenate([other, own], axis),
    )


def half(value, bit, axis):
    size = value.shape[axis] // 2
    return lax.dynamic_slice_in_dim(value, bit * size, size, axis)


def trade(value, axes):
    return lax.all_to_all(value, axes, split_axis=0, concat_axis=0, tiled=True)


def copies(value, n):
    return jnp.broadcast_to(value[None], (n,) + value.shape)


def over_ze(value):
    if lax.axis_size("ze") == 1:
        return value
    return lax.all_gather(value, "ze", axis=0, tiled=True)


def total_ze(value):
    if lax.axis_size("ze") == 1:
        return value
    return lax.psum_scatter(value.astype(BF), "ze", scatter_dimension=0, tiled=True).astype(F32)


def cut(w):
    r, k = w.shape[0], w.shape[1] // 4

    def body(w_ref, out_ref):
        out_ref[0] = w_ref[...]

    return pl.pallas_call(
        body,
        grid=(8,),
        in_specs=[pl.BlockSpec((r, k), lambda i: (0, i % 4))],
        out_specs=pl.BlockSpec((1, r, k), lambda i: (i, 0, 0)),
        out_shape=jax.ShapeDtypeStruct((8, r, k), w.dtype),
        cost_estimate=pl.CostEstimate(flops=0, bytes_accessed=24 * r * k, transcendentals=0),
    )(w)


def fold(t):
    r, k = t.shape[1:]

    def body(a_ref, b_ref, out_ref):
        out_ref[...] = a_ref[0].astype(F32) + b_ref[0].astype(F32)

    return pl.pallas_call(
        body,
        grid=(4,),
        in_specs=[
            pl.BlockSpec((1, r, k), lambda i: (i, 0, 0)),
            pl.BlockSpec((1, r, k), lambda i: (i + 4, 0, 0)),
        ],
        out_specs=pl.BlockSpec((r, k), lambda i: (0, i)),
        out_shape=jax.ShapeDtypeStruct((r, 4 * k), F32),
        cost_estimate=pl.CostEstimate(flops=0, bytes_accessed=32 * r * k, transcendentals=0),
    )(t, t)


class Place:
    def __init__(self, width):
        self.zh = lax.axis_index("zh")
        self.zl = lax.axis_index("zl")
        self.x = lax.axis_index("x")
        self.y = lax.axis_index("y")
        self.c = lax.axis_index("c")
        self.ze = lax.axis_size("ze")
        self.rows = width // (self.ze * 8)
        self.line = []
        self.first = []

    def ordered(self, value, axes):
        if self.line:
            value = after(value, self.line[-1])
        if self.first:
            value = after(value, tuple(self.first))
            self.first = []
        self.line.append(trade(value, axes))
        return self.line[-1]

    def gather(self, w):
        r, k = w.shape
        w = self.ordered(cut(w), GROUP)
        w = over_ze(w.reshape(8 * r, k // 4))
        own = lax.all_gather(w, "x", axis=1, tiled=True)
        return own, swap(own, "c")

    def open_grad(self, left, far):
        part = dot_tn(left, far).astype(BF)
        return part, swap(part, "c")

    def close_grad(self, left, own, got):
        part = (dot_tn(left, own) + got.astype(F32)).astype(BF)
        t = lax.psum_scatter(part, "x", scatter_dimension=1, tiled=True)
        t = total_ze(t).astype(BF).reshape(8, self.rows, -1)
        return part, fold(self.ordered(t, GROUP))

    def gather_rows(self, w, swapped=False):
        a = self.ordered(copies(w, 4), ("zh", "zl"))
        a = over_ze(a)
        if swapped:
            return in_order(self.y, a, swap(a, "y"), 1).reshape(-1, w.shape[1])
        return lax.all_gather(a, "y", axis=1, tiled=True).reshape(-1, w.shape[1])

    def scatter_rows(self, left, right):
        part = dot_tn(left, right).astype(BF)
        t = part.reshape(-1, 2 * self.rows, right.shape[1])
        t = lax.psum_scatter(t, "y", scatter_dimension=1, tiled=True)
        t = self.ordered(total_ze(t).astype(BF), ("zh", "zl")).astype(F32)
        return part, (t[0] + t[1]) + (t[2] + t[3])

    def spread(self, v):
        h = v.shape[1] // 2
        vy = swap(v, "y")
        vz = swap(v, "zl")
        both = jnp.concatenate([swap(vz[:, :h], "y"), swap(vy[:, h:], "zl")], 1)
        return jnp.concatenate([v, vy, vz, both], 0)

    def collect(self, part):
        t, d = part.shape
        h = d // 2
        part = part.reshape(4, t // 4, d)
        a, b = part[..., :h], part[..., h:]
        got_a = swap(a[2:].astype(BF), "zl").astype(F32)
        got_b = swap(b[1::2].astype(BF), "y").astype(F32)
        a_y = (a[1] + got_a[1]).astype(BF)
        b_z = (b[2] + got_b[1]).astype(BF)
        a0 = a[0] + got_a[0] + swap(a_y, "y").astype(F32)
        b0 = b[0] + got_b[0] + swap(b_z, "zl").astype(F32)
        return jnp.concatenate([a0, b0], 1)

    def own_rows(self, v):
        mb, t, d = v.shape
        v = v.reshape(mb, 4, t // 4, d)
        v = lax.dynamic_slice_in_dim(v, self.x * 2 + self.c, 1, 1)
        return v.reshape(mb * t // 4, d)

    def spread_tp(self, v, mb):
        d = v.shape[1]
        v = v.reshape(mb, 1, -1, d)
        pair = in_order(self.x, v, swap(v, "x"), 1)[:, :, None]
        full = in_order(self.c, pair, swap(pair, "c"), 2)
        return full.reshape(mb, -1, d)

    def collect_tp(self, part, mb):
        t, d = part.shape
        part = part.reshape(mb, 2, 2, t // (4 * mb), d)
        mine = half(part, self.c, 2)
        mine = mine + swap(half(part, 1 - self.c, 2).astype(BF), "c").astype(F32)
        own = half(mine, self.x, 1)
        own = own + swap(half(mine, 1 - self.x, 1).astype(BF), "x").astype(F32)
        return own.reshape(t // 4, d)

    def trade_half(self, v, bit, axis, name):
        return jnp.stack([half(v, bit, axis), swap(half(v, 1 - bit, axis), name)])

    def memory_in(self, m):
        mb, t, k = m.shape
        v = m.reshape(mb, 2, 2, t // 4, 2, 2, k // 4).transpose(4, 5, 1, 2, 0, 3, 6)
        v = self.trade_half(v, self.c, 3, "c")
        v = self.trade_half(v, self.x, 3, "x")
        v = jnp.where(self.x == 1, jnp.flip(v, 0), v)
        v = self.trade_half(v, self.y, 3, "y")
        v = self.trade_half(v, self.zl, 3, "zl")
        v = v.reshape(2, 2, 2, 2, mb * t // 4, k // 4)
        v = v.transpose(3, 0, 1, 4, 2, 5).reshape(2, mb * t, k // 2)
        return v[0], v[1]

    def memory_out(self, own, far, mb):
        t, k = own.shape[0], own.shape[1] * 2
        v = jnp.stack([own, far]).astype(BF).reshape(2, 2, 2, t // 4, 2, k // 4)
        v = v.transpose(0, 4, 1, 2, 3, 5)
        v = in_order(self.zl, v[:, :, :1], swap(v[:, :, 1:], "zl"), 2)
        v = in_order(self.y, v[:, :, :, :1], swap(v[:, :, :, 1:], "y"), 3)
        v = in_order(self.c, v[:1][None], swap(v[1:], "c")[None], 0)
        v = v[:, 0]
        v = in_order(self.x, half(v, self.x, 1)[None], swap(half(v, 1 - self.x, 1), "x")[None], 0)
        v = v.reshape(2, 2, 2, 2, mb, t // (4 * mb), k // 4)
        return v.transpose(4, 0, 1, 5, 2, 3, 6).reshape(mb, t // mb, k).astype(F32)


def rms(v, g):
    r = lax.rsqrt(jnp.mean(v * v, axis=-1, keepdims=True) + EPS)
    return v * r * g


def rms_back(v, g, dn):
    r = lax.rsqrt(jnp.mean(v * v, axis=-1, keepdims=True) + EPS)
    gain = jnp.sum(dn * v * r, axis=0)
    gd = g * dn
    return r * gd - v * (r * r * r) * jnp.mean(v * gd, axis=-1, keepdims=True), gain


def silu_parts(v):
    s = jax.nn.sigmoid(v)
    return v * s, s * (1.0 + v * (1.0 - s))


def exchange(v):
    here = lax.axis_index(GROUP)
    out = []
    for k in range(8):
        block = lax.dynamic_index_in_dim(v, here ^ k, 0, keepdims=False)
        out.append(block if k == 0 else lax.ppermute(block, GROUP, [(i, i ^ k) for i in range(8)]))
    return out


def to_pairs(v):
    n, mb, t, k = v.shape
    v = v.reshape(n, mb, t, k // HD, HD).transpose(1, 3, 0, 2, 4).reshape(-1, n, t, HD)
    return jnp.concatenate(exchange(v), 1)


def from_pairs(v, mb, t):
    n = v.shape[0]
    here = lax.axis_index(GROUP)
    v = v.reshape(n, 8, t, HD)
    got = [v[:, 0]]
    for k in range(1, 8):
        got.append(lax.ppermute(v[:, k], GROUP, [(i, i ^ k) for i in range(8)]))
    v = jnp.stack(got)
    v = jnp.stack([lax.dynamic_index_in_dim(v, here ^ k, 0, keepdims=False) for k in range(8)])
    return v.reshape(mb, -1, n, t, HD).transpose(2, 0, 3, 1, 4).reshape(n, mb, t, -1)


def positions(order, ids, group_len):
    slots = jnp.arange(order.shape[0], dtype=jnp.int32)
    group = jnp.sum(
        jnp.where((ids // group_len)[:, None] == slots[None, :], order[None, :], 0), axis=1
    )
    return group * group_len + ids % group_len


def shards(
    stream_in,
    cache_keys,
    cache_values,
    memory,
    cotangent,
    query_proj,
    output_proj,
    gate_first,
    up_first,
    down_first,
    memory_in,
    memory_out,
    gate_second,
    up_second,
    down_second,
    norm_gains,
    group_order,
    seq_lengths,
):
    mb, tok, width = stream_in.shape
    at = Place(width)
    scaling = HD ** (-0.5)
    groups = group_order.shape[0]
    tokens = tok * at.ze * 8
    group_len = tokens // groups

    gains = norm_gains
    stream = stream_in
    r0 = at.own_rows(stream).astype(F32)

    wq = at.gather_rows(query_proj)
    cache = to_pairs(jnp.stack([cache_keys, cache_values], 0))
    keys, values = over_ze(cache[0]), over_ze(cache[1])
    g1 = at.gather(gate_first)
    u1 = at.gather(up_first)
    wo = at.gather_rows(output_proj, True)
    n1 = rms(stream.astype(F32).reshape(mb * tok, width), gains[0]).astype(BF)
    q = to_pairs(dot(n1, wq).astype(BF).reshape(1, mb, tok, -1))[0]
    at.first = [q]
    d1 = at.gather(down_first)

    pair = lax.axis_index(("zh", "zl", "y"))
    heads = cache_keys.shape[2] // HD
    batch = pair // heads
    length = lax.dynamic_slice_in_dim(seq_lengths, batch, 1, 0)
    q_rows = q.shape[0]
    k_rows = keys.shape[0]
    rows = jnp.arange(k_rows, dtype=jnp.int32)
    ids = rows // q_rows * q_rows + (rows % q_rows // tok ^ pair) * tok + rows % tok
    k_pos = positions(group_order, ids, group_len)
    q_pos = lax.dynamic_slice_in_dim(k_pos, lax.axis_index("ze") * q_rows, q_rows, 0)
    allowed = (k_pos[None, :] <= q_pos[:, None]) & (k_pos < length)[None, :]
    s = jnp.where(allowed, dot_nt(q, keys) * scaling, FILL)
    top = jnp.max(s, axis=1, keepdims=True)
    e = jnp.exp(s - top)
    total = jnp.sum(e, axis=1, keepdims=True)
    o = dot(e.astype(BF), values) / total
    lse = top + jnp.log(total)
    attn = from_pairs(o.astype(BF)[None], mb, tok).reshape(mb * tok, -1)

    at.first = [attn]
    mi, mo = at.gather(memory_in), at.gather(memory_out)
    x1 = r0 + at.collect_tp(dot_nt(attn, wo), mb)
    at.first = [x1]
    g2 = at.gather(gate_second)

    def ffn(x, gain, wg, wu, wd, pins):
        n = after(at.spread(rms(x, gain).astype(BF)), pins)
        gate = [dot(n, w) for w in wg]
        up = [dot(n, w) for w in wu]
        hidden = [(jax.nn.silu(g) * u).astype(BF) for g, u in zip(gate, up)]
        out = at.collect(dot_nt(hidden[0], wd[0]) + dot_nt(hidden[1], wd[1]))
        return x + out, (n, gate, up, hidden)

    x2, kept1 = ffn(x1, gains[1], g1, u1, d1, ())
    at.first = [kept1[0]]
    u2 = at.gather(up_second)
    d2 = at.gather(down_second)

    x2 = held(x2, at.line[9])
    mem = at.memory_in(memory)
    n3 = at.spread(rms(x2, gains[2]).astype(BF))
    za = [dot(n3, w) for w in mi]
    gm = [(m.astype(F32) * jax.nn.silu(z)).astype(BF) for m, z in zip(mem, za)]
    x3 = x2 + at.collect(dot_nt(gm[0], mo[0]) + dot_nt(gm[1], mo[1]))

    x4, kept2 = ffn(x3, gains[3], g2, u2, d2, ())
    stream_out = at.spread_tp(x4.astype(BF), mb)

    cot = at.own_rows(cotangent)
    yb = at.spread(cot)

    zline = at.line

    def ffn_back(y, kept, wg, wu, wd, pins):
        n, gate, up, hidden = kept
        far_d, got_d = at.open_grad(y, hidden[1])
        y2 = after(y, far_d)
        dg, du = [], []
        for g, u, w in zip(gate, up, wd):
            dh = dot(y2, w)
            act, slope = silu_parts(g)
            dg.append((dh * u * slope).astype(BF))
            du.append((dh * act).astype(BF))
        part_d, down_grad = at.close_grad(y, hidden[0], got_d)
        dg, du = after((dg, du), (part_d,) + pins)
        dn = dot_nt(dg[0], wg[0]) + dot_nt(dg[1], wg[1])
        dn = dn + dot_nt(du[0], wu[0]) + dot_nt(du[1], wu[1])
        far_g, got_g = at.open_grad(n, dg[1])
        far_u, got_u = at.open_grad(n, du[1])
        dn = after(at.collect(dn), (far_g, far_u))
        return dn, down_grad, (n, dg[0], got_g), (n, du[0], got_u)

    dn4, down_second_grad, open_g, open_u = ffn_back(yb, kept2, g2, u2, d2, ())
    back, gain4 = rms_back(x3, gains[3], dn4)
    dx3 = cot.astype(F32) + back

    part_g, gate_second_grad = at.close_grad(*open_g)
    yg = after(at.spread(dx3.astype(BF)), part_g)
    part_u, up_second_grad = at.close_grad(*open_u)
    far, got = at.open_grad(yg, gm[1])
    dz, dm = [], []
    for w, z, m in zip(mo, za, mem):
        dgm = dot(yg, w)
        act, slope = silu_parts(z)
        dm.append(dgm * act)
        dz.append((dgm * m.astype(F32) * slope).astype(BF))
    dz = after(dz, (part_u, far))
    dn3 = dot_nt(dz[0], mi[0]) + dot_nt(dz[1], mi[1])
    part_o, memory_out_grad = at.close_grad(yg, gm[0], got)
    far, got = at.open_grad(n3, dz[1])
    dn3 = after(at.collect(dn3), (part_o, far, zline[10]))
    memory_grad = at.memory_out(dm[0], dm[1], mb)
    back, gain3 = rms_back(x2, gains[2], dn3)
    dx2 = dx3 + back

    part_i, memory_in_grad = at.close_grad(n3, dz[0], got)
    ya = after(at.spread(dx2.astype(BF)), (part_i, zline[11]))
    dn2, down_first_grad, open_g, open_u = ffn_back(ya, kept1, g1, u1, d1, (zline[12],))
    dn2 = after(dn2, (zline[13], zline[14]))
    back, gain2 = rms_back(x1, gains[1], dn2)
    dx1 = dx2 + back

    part_g, gate_first_grad = at.close_grad(*open_g)
    yo = after(at.spread_tp(dx1.astype(BF), mb), (part_g, zline[15])).reshape(mb * tok, width)
    part_u, up_first_grad = at.close_grad(*open_u)
    do = to_pairs(dot(yo, wo).astype(BF).reshape(1, mb, tok, -1))[0]
    do = after(do, part_u)
    part_w, output_grad = at.scatter_rows(yo, attn)
    delta = jnp.sum(do.astype(F32) * o, axis=1, keepdims=True)
    p = jnp.exp(s - lse)
    ds = (p * (dot_nt(do, values) - delta)).astype(BF)
    dq = after((dot(ds, keys) * scaling).astype(BF)[None], (part_w, zline[16]))
    dq = from_pairs(held(dq, zline[16]), mb, tok)
    dk = total_ze(dot_tn(ds, q) * scaling).astype(BF)
    dv = total_ze(dot_tn(p.astype(BF), do)).astype(BF)
    dkv = from_pairs(held(jnp.stack([dk, dv]), dq), mb, tok).astype(F32)
    keys_grad, values_grad = dkv[0], dkv[1]
    dq = dq.reshape(mb * tok, -1)
    dn1 = at.collect_tp(held(dot_nt(dq, wq), zline[17]), mb)
    _, query_grad = at.scatter_rows(n1, dq)
    back, gain1 = rms_back(r0, gains[0], dn1)
    stream_grad = at.spread_tp((dx1 + back).astype(BF), mb).astype(F32)

    gain = jnp.stack([gain1, gain2, gain3, gain4])
    for axis in ("c", "x", "y", "zh", "zl"):
        gain = gain + swap(gain, axis)
    if at.ze > 1:
        gain = lax.psum(gain, "ze")
    spot = lax.axis_index(SEQ)
    gains_grad = lax.dynamic_slice_in_dim(gain, spot * at.rows, at.rows, 1)

    return (
        stream_out,
        stream_grad,
        keys_grad,
        values_grad,
        memory_grad,
        query_grad,
        output_grad,
        gate_first_grad,
        up_first_grad,
        down_first_grad,
        memory_in_grad,
        memory_out_grad,
        gate_second_grad,
        up_second_grad,
        down_second_grad,
        gains_grad,
    )


def solution(mesh):
    seq, tp = mesh.shape["seq"], mesh.shape["tp"]
    fine = Mesh(
        mesh.devices.reshape(seq // 8, 2, 2, 2, tp // 2, 2), ("ze", "zh", "zl", "y", "x", "c")
    )
    tokens = P(None, SEQ, None)
    both = P(None, SEQ, TP)
    weight = P(SEQ, TP)
    return jax.shard_map(
        shards,
        mesh=fine,
        in_specs=(tokens, both, both, both, tokens) + (weight,) * 10 + (P(), P(), P()),
        out_specs=(tokens, tokens, both, both, both) + (weight,) * 10 + (P(None, SEQ),),
        check_vma=False,
    )
```

```python
import jax
import jax.numpy as jnp
from jax import lax
from jax.experimental import pallas as pl
from jax.sharding import Mesh
from jax.sharding import PartitionSpec as P

HD = 128
EPS = 1e-05
FILL = -1e30
BF = jnp.bfloat16
F32 = jnp.float32
SEQ = ("ze", "zh", "zl", "y")
TP = ("x", "c")
GROUP = ("zh", "zl", "y")
UNIT = ("zl", "y", "x", "c")


def swap(value, axis):
    return lax.ppermute(value, axis, [(0, 1), (1, 0)])


def after(value, earlier):
    return lax.optimization_barrier((value, earlier))[0]


def held(value, *earlier):
    earlier = jax.tree.leaves(earlier)
    if not earlier:
        return value
    anywhere = pl.BlockSpec(memory_space=pl.ANY)

    def body(*refs):
        pass

    return pl.pallas_call(
        body,
        in_specs=[anywhere] * (1 + len(earlier)),
        out_specs=anywhere,
        out_shape=jax.ShapeDtypeStruct(value.shape, value.dtype),
        input_output_aliases={0: 0},
        cost_estimate=pl.CostEstimate(flops=0, bytes_accessed=0, transcendentals=0),
    )(value, *earlier)


def dot(a, b):
    return jnp.dot(a, b, preferred_element_type=F32)


def dot_nt(a, b):
    return lax.dot_general(a, b, (((1,), (1,)), ((), ())), preferred_element_type=F32)


def dot_tn(a, b):
    return lax.dot_general(a, b, (((0,), (0,)), ((), ())), preferred_element_type=F32)


def in_order(bit, own, other, axis):
    return jnp.where(
        bit == 0,
        jnp.concatenate([own, other], axis),
        jnp.concatenate([other, own], axis),
    )


def half(value, bit, axis):
    size = value.shape[axis] // 2
    return lax.dynamic_slice_in_dim(value, bit * size, size, axis)


def trade(value, axes):
    return lax.all_to_all(value, axes, split_axis=0, concat_axis=0, tiled=True)


def copies(value, n):
    return jnp.broadcast_to(value[None], (n,) + value.shape)


def over_ze(value):
    if lax.axis_size("ze") == 1:
        return value
    return lax.all_gather(value, "ze", axis=0, tiled=True)


def total_ze(value):
    if lax.axis_size("ze") == 1:
        return value
    return lax.psum_scatter(value.astype(BF), "ze", scatter_dimension=0, tiled=True).astype(F32)


def cut(w):
    r, k = w.shape[0], w.shape[1] // 4

    def body(w_ref, out_ref):
        out_ref[0] = w_ref[...]

    return pl.pallas_call(
        body,
        grid=(8,),
        in_specs=[pl.BlockSpec((r, k), lambda i: (0, i % 4))],
        out_specs=pl.BlockSpec((1, r, k), lambda i: (i, 0, 0)),
        out_shape=jax.ShapeDtypeStruct((8, r, k), w.dtype),
        cost_estimate=pl.CostEstimate(flops=0, bytes_accessed=24 * r * k, transcendentals=0),
    )(w)


def fold(t):
    r, k = t.shape[1:]

    def body(a_ref, b_ref, out_ref):
        out_ref[...] = a_ref[0].astype(F32) + b_ref[0].astype(F32)

    return pl.pallas_call(
        body,
        grid=(4,),
        in_specs=[
            pl.BlockSpec((1, r, k), lambda i: (i, 0, 0)),
            pl.BlockSpec((1, r, k), lambda i: (i + 4, 0, 0)),
        ],
        out_specs=pl.BlockSpec((r, k), lambda i: (0, i)),
        out_shape=jax.ShapeDtypeStruct((r, 4 * k), F32),
        cost_estimate=pl.CostEstimate(flops=0, bytes_accessed=32 * r * k, transcendentals=0),
    )(t, t)


class Place:
    def __init__(self, width):
        self.zh = lax.axis_index("zh")
        self.zl = lax.axis_index("zl")
        self.x = lax.axis_index("x")
        self.y = lax.axis_index("y")
        self.c = lax.axis_index("c")
        self.ze = lax.axis_size("ze")
        self.rows = width // (self.ze * 8)
        self.line = []
        self.first = []

    def ordered(self, value, axes):
        if self.line:
            value = after(value, self.line[-1])
        if self.first:
            value = after(value, tuple(self.first))
            self.first = []
        self.line.append(trade(value, axes))
        return self.line[-1]

    def gather(self, w):
        r, k = w.shape
        w = self.ordered(cut(w), GROUP)
        w = over_ze(w.reshape(8 * r, k // 4))
        own = lax.all_gather(w, "x", axis=1, tiled=True)
        return own, swap(own, "c")

    def open_grad(self, left, far):
        part = dot_tn(left, far).astype(BF)
        return part, swap(part, "c")

    def close_grad(self, left, own, got):
        part = (dot_tn(left, own) + got.astype(F32)).astype(BF)
        t = lax.psum_scatter(part, "x", scatter_dimension=1, tiled=True)
        t = total_ze(t).astype(BF).reshape(8, self.rows, -1)
        return part, fold(self.ordered(t, GROUP))

    def gather_rows(self, w, swapped=False):
        a = self.ordered(copies(w, 4), ("zh", "zl"))
        a = over_ze(a)
        if swapped:
            return in_order(self.y, a, swap(a, "y"), 1).reshape(-1, w.shape[1])
        return lax.all_gather(a, "y", axis=1, tiled=True).reshape(-1, w.shape[1])

    def scatter_rows(self, left, right, swapped=False):
        part = dot_tn(left, right).astype(BF)
        t = part.reshape(-1, 2 * self.rows, right.shape[1])
        if swapped:
            got = swap(half(t, 1 - self.y, 1), "y")
            t = half(t, self.y, 1).astype(F32) + got.astype(F32)
        else:
            t = lax.psum_scatter(t, "y", scatter_dimension=1, tiled=True)
        t = self.ordered(total_ze(t).astype(BF), ("zh", "zl")).astype(F32)
        return part, (t[0] + t[1]) + (t[2] + t[3])

    def spread(self, v):
        h = v.shape[1] // 2
        vy = swap(v, "y")
        vz = swap(v, "zl")
        both = jnp.concatenate([swap(vz[:, :h], "y"), swap(vy[:, h:], "zl")], 1)
        return jnp.concatenate([v, vy, vz, both], 0)

    def collect(self, part):
        t, d = part.shape
        h = d // 2
        part = part.reshape(4, t // 4, d)
        a, b = part[..., :h], part[..., h:]
        got_a = swap(a[2:].astype(BF), "zl").astype(F32)
        got_b = swap(b[1::2].astype(BF), "y").astype(F32)
        a_y = (a[1] + got_a[1]).astype(BF)
        b_z = (b[2] + got_b[1]).astype(BF)
        a0 = a[0] + got_a[0] + swap(a_y, "y").astype(F32)
        b0 = b[0] + got_b[0] + swap(b_z, "zl").astype(F32)
        return jnp.concatenate([a0, b0], 1)

    def own_rows(self, v):
        mb, t, d = v.shape
        v = v.reshape(mb, 4, t // 4, d)
        v = lax.dynamic_slice_in_dim(v, self.x * 2 + self.c, 1, 1)
        return v.reshape(mb * t // 4, d)

    def spread_tp(self, v, mb):
        d = v.shape[1]
        v = v.reshape(mb, 1, -1, d)
        pair = in_order(self.x, v, swap(v, "x"), 1)[:, :, None]
        full = in_order(self.c, pair, swap(pair, "c"), 2)
        return full.reshape(mb, -1, d)

    def collect_tp(self, part, mb):
        t, d = part.shape
        part = part.reshape(mb, 2, 2, t // (4 * mb), d)
        mine = half(part, self.c, 2)
        mine = mine + swap(half(part, 1 - self.c, 2).astype(BF), "c").astype(F32)
        own = half(mine, self.x, 1)
        own = own + swap(half(mine, 1 - self.x, 1).astype(BF), "x").astype(F32)
        return own.reshape(t // 4, d)

    def trade_half(self, v, bit, axis, name):
        return jnp.stack([half(v, bit, axis), swap(half(v, 1 - bit, axis), name)])

    def memory_in(self, m):
        mb, t, k = m.shape
        v = m.reshape(mb, 2, 2, t // 4, 2, 2, k // 4).transpose(4, 5, 1, 2, 0, 3, 6)
        v = self.trade_half(v, self.c, 3, "c")
        v = self.trade_half(v, self.x, 3, "x")
        v = jnp.where(self.x == 1, jnp.flip(v, 0), v)
        v = self.trade_half(v, self.y, 3, "y")
        v = self.trade_half(v, self.zl, 3, "zl")
        v = v.reshape(2, 2, 2, 2, mb * t // 4, k // 4)
        v = v.transpose(3, 0, 1, 4, 2, 5).reshape(2, mb * t, k // 2)
        return v[0], v[1]

    def memory_out(self, own, far, mb):
        t, k = own.shape[0], own.shape[1] * 2
        v = jnp.stack([own, far]).astype(BF).reshape(2, 2, 2, t // 4, 2, k // 4)
        v = v.transpose(0, 4, 1, 2, 3, 5)
        v = in_order(self.zl, v[:, :, :1], swap(v[:, :, 1:], "zl"), 2)
        v = in_order(self.y, v[:, :, :, :1], swap(v[:, :, :, 1:], "y"), 3)
        v = in_order(self.c, v[:1][None], swap(v[1:], "c")[None], 0)
        v = v[:, 0]
        v = in_order(self.x, half(v, self.x, 1)[None], swap(half(v, 1 - self.x, 1), "x")[None], 0)
        v = v.reshape(2, 2, 2, 2, mb, t // (4 * mb), k // 4)
        return v.transpose(4, 0, 1, 5, 2, 3, 6).reshape(mb, t // mb, k).astype(F32)


def rms(v, g):
    r = lax.rsqrt(jnp.mean(v * v, axis=-1, keepdims=True) + EPS)
    return v * r * g


def rms_back(v, g, dn):
    r = lax.rsqrt(jnp.mean(v * v, axis=-1, keepdims=True) + EPS)
    gain = jnp.sum(dn * v * r, axis=0)
    gd = g * dn
    return r * gd - v * (r * r * r) * jnp.mean(v * gd, axis=-1, keepdims=True), gain


def silu_parts(v):
    s = jax.nn.sigmoid(v)
    return v * s, s * (1.0 + v * (1.0 - s))


def exchange(v):
    here = lax.axis_index(GROUP)
    out = []
    for k in range(8):
        block = lax.dynamic_index_in_dim(v, here ^ k, 0, keepdims=False)
        out.append(block if k == 0 else lax.ppermute(block, GROUP, [(i, i ^ k) for i in range(8)]))
    return out


def to_pairs(v):
    n, mb, t, k = v.shape
    v = v.reshape(n, mb, t, k // HD, HD).transpose(1, 3, 0, 2, 4).reshape(-1, n, t, HD)
    return jnp.concatenate(exchange(v), 1)


def from_pairs(v, mb, t):
    n = v.shape[0]
    here = lax.axis_index(GROUP)
    v = v.reshape(n, 8, t, HD)
    got = [v[:, 0]]
    for k in range(1, 8):
        got.append(lax.ppermute(v[:, k], GROUP, [(i, i ^ k) for i in range(8)]))
    v = jnp.stack(got)
    v = jnp.stack([lax.dynamic_index_in_dim(v, here ^ k, 0, keepdims=False) for k in range(8)])
    return v.reshape(mb, -1, n, t, HD).transpose(2, 0, 3, 1, 4).reshape(n, mb, t, -1)


def positions(order, ids, group_len):
    slots = jnp.arange(order.shape[0], dtype=jnp.int32)
    group = jnp.sum(
        jnp.where((ids // group_len)[:, None] == slots[None, :], order[None, :], 0), axis=1
    )
    return group * group_len + ids % group_len


def shards(
    stream_in,
    cache_keys,
    cache_values,
    memory,
    cotangent,
    query_proj,
    output_proj,
    gate_first,
    up_first,
    down_first,
    memory_in,
    memory_out,
    gate_second,
    up_second,
    down_second,
    norm_gains,
    group_order,
    seq_lengths,
):
    mb, tok, width = stream_in.shape
    at = Place(width)
    scaling = HD ** (-0.5)
    groups = group_order.shape[0]
    tokens = tok * at.ze * 8
    group_len = tokens // groups

    gains = norm_gains
    stream = stream_in
    r0 = at.own_rows(stream).astype(F32)

    wq = at.gather_rows(query_proj)
    cache = to_pairs(jnp.stack([cache_keys, cache_values], 0))
    keys, values = over_ze(cache[0]), over_ze(cache[1])
    g1 = at.gather(gate_first)
    u1 = at.gather(up_first)
    wo = at.gather_rows(output_proj, True)
    n1 = rms(stream.astype(F32).reshape(mb * tok, width), gains[0]).astype(BF)
    q = to_pairs(dot(n1, wq).astype(BF).reshape(1, mb, tok, -1))[0]
    at.first = [q]
    d1 = at.gather(down_first)

    pair = lax.axis_index(("zh", "zl", "y"))
    heads = cache_keys.shape[2] // HD
    batch = pair // heads
    length = lax.dynamic_slice_in_dim(seq_lengths, batch, 1, 0)
    q_rows = q.shape[0]
    k_rows = keys.shape[0]
    rows = jnp.arange(k_rows, dtype=jnp.int32)
    ids = rows // q_rows * q_rows + (rows % q_rows // tok ^ pair) * tok + rows % tok
    k_pos = positions(group_order, ids, group_len)
    q_pos = lax.dynamic_slice_in_dim(k_pos, lax.axis_index("ze") * q_rows, q_rows, 0)
    allowed = (k_pos[None, :] <= q_pos[:, None]) & (k_pos < length)[None, :]
    s = jnp.where(allowed, dot_nt(q, keys) * scaling, FILL)
    top = jnp.max(s, axis=1, keepdims=True)
    e = jnp.exp(s - top)
    total = jnp.sum(e, axis=1, keepdims=True)
    o = dot(e.astype(BF), values) / total
    lse = top + jnp.log(total)
    attn = from_pairs(o.astype(BF)[None], mb, tok).reshape(mb * tok, -1)

    at.first = [attn]
    mi, mo = at.gather(memory_in), at.gather(memory_out)
    x1 = r0 + at.collect_tp(dot_nt(attn, wo), mb)
    at.first = [x1]
    g2 = at.gather(gate_second)

    def ffn(x, gain, wg, wu, wd, pins):
        n = after(at.spread(rms(x, gain).astype(BF)), pins)
        gate = [dot(n, w) for w in wg]
        up = [dot(n, w) for w in wu]
        hidden = [(jax.nn.silu(g) * u).astype(BF) for g, u in zip(gate, up)]
        out = at.collect(dot_nt(hidden[0], wd[0]) + dot_nt(hidden[1], wd[1]))
        return x + out, (n, gate, up, hidden)

    x2, kept1 = ffn(x1, gains[1], g1, u1, d1, ())
    at.first = [kept1[0]]
    u2 = at.gather(up_second)
    d2 = at.gather(down_second)

    x2 = held(x2, at.line[9])
    mem = at.memory_in(memory)
    n3 = at.spread(rms(x2, gains[2]).astype(BF))
    za = [dot(n3, w) for w in mi]
    gm = [(m.astype(F32) * jax.nn.silu(z)).astype(BF) for m, z in zip(mem, za)]
    x3 = x2 + at.collect(dot_nt(gm[0], mo[0]) + dot_nt(gm[1], mo[1]))

    x4, kept2 = ffn(x3, gains[3], g2, u2, d2, ())
    stream_out = at.spread_tp(x4.astype(BF), mb)

    cot = at.own_rows(cotangent)
    yb = at.spread(cot)

    zline = at.line

    def ffn_back(y, kept, wg, wu, wd, pins):
        n, gate, up, hidden = kept
        far_d, got_d = at.open_grad(y, hidden[1])
        y2 = after(y, far_d)
        dg, du = [], []
        for g, u, w in zip(gate, up, wd):
            dh = dot(y2, w)
            act, slope = silu_parts(g)
            dg.append((dh * u * slope).astype(BF))
            du.append((dh * act).astype(BF))
        part_d, down_grad = at.close_grad(y, hidden[0], got_d)
        dg, du = after((dg, du), (part_d,) + pins)
        dn = dot_nt(dg[0], wg[0]) + dot_nt(dg[1], wg[1])
        dn = dn + dot_nt(du[0], wu[0]) + dot_nt(du[1], wu[1])
        far_g, got_g = at.open_grad(n, dg[1])
        far_u, got_u = at.open_grad(n, du[1])
        dn = after(at.collect(dn), (far_g, far_u))
        return dn, down_grad, (n, dg[0], got_g), (n, du[0], got_u)

    dn4, down_second_grad, open_g, open_u = ffn_back(yb, kept2, g2, u2, d2, ())
    back, gain4 = rms_back(x3, gains[3], dn4)
    dx3 = cot.astype(F32) + back

    part_g, gate_second_grad = at.close_grad(*open_g)
    yg = after(at.spread(dx3.astype(BF)), part_g)
    part_u, up_second_grad = at.close_grad(*open_u)
    far, got = at.open_grad(yg, gm[1])
    dz, dm = [], []
    for w, z, m in zip(mo, za, mem):
        dgm = dot(yg, w)
        act, slope = silu_parts(z)
        dm.append(dgm * act)
        dz.append((dgm * m.astype(F32) * slope).astype(BF))
    dz = after(dz, (part_u, far))
    dn3 = dot_nt(dz[0], mi[0]) + dot_nt(dz[1], mi[1])
    part_o, memory_out_grad = at.close_grad(yg, gm[0], got)
    far, got = at.open_grad(n3, dz[1])
    dn3 = after(at.collect(dn3), (part_o, far, zline[10]))
    memory_grad = at.memory_out(dm[0], dm[1], mb)
    back, gain3 = rms_back(x2, gains[2], dn3)
    dx2 = held(dx3 + back, zline[11])

    part_i, memory_in_grad = at.close_grad(n3, dz[0], got)
    ya = after(at.spread(dx2.astype(BF)), (part_i, zline[11]))
    dn2, down_first_grad, open_g, open_u = ffn_back(ya, kept1, g1, u1, d1, (zline[12],))
    dn2 = after(dn2, (zline[13], zline[14]))
    back, gain2 = rms_back(x1, gains[1], dn2)
    dx1 = held(dx2 + back, zline[15])

    part_g, gate_first_grad = at.close_grad(*open_g)
    yo = after(at.spread_tp(dx1.astype(BF), mb), (part_g, zline[15])).reshape(mb * tok, width)
    part_u, up_first_grad = at.close_grad(*open_u)
    do = to_pairs(dot(yo, wo).astype(BF).reshape(1, mb, tok, -1))[0]
    do = after(do, part_u)
    part_w, output_grad = at.scatter_rows(yo, attn)
    do = held(do, zline[16])
    delta = jnp.sum(do.astype(F32) * o, axis=1, keepdims=True)
    p = jnp.exp(s - lse)
    ds = (p * (dot_nt(do, values) - delta)).astype(BF)
    dq = after((dot(ds, keys) * scaling).astype(BF)[None], (part_w, zline[16]))
    dq = from_pairs(dq, mb, tok)
    dk = total_ze(dot_tn(ds, q) * scaling).astype(BF)
    dv = total_ze(dot_tn(p.astype(BF), do)).astype(BF)
    dkv = from_pairs(held(jnp.stack([dk, dv]), dq), mb, tok).astype(F32)
    keys_grad, values_grad = dkv[0], dkv[1]
    dq = dq.reshape(mb * tok, -1)
    dn1 = at.collect_tp(held(dot_nt(dq, wq), zline[17]), mb)
    _, query_grad = at.scatter_rows(n1, dq, True)
    back, gain1 = rms_back(r0, gains[0], dn1)
    stream_grad = at.spread_tp((dx1 + back).astype(BF), mb).astype(F32)

    gain = jnp.stack([gain1, gain2, gain3, gain4])
    for axis in ("c", "x", "y", "zh", "zl"):
        gain = gain + swap(gain, axis)
    if at.ze > 1:
        gain = lax.psum(gain, "ze")
    spot = lax.axis_index(SEQ)
    gains_grad = lax.dynamic_slice_in_dim(gain, spot * at.rows, at.rows, 1)

    return (
        stream_out,
        stream_grad,
        keys_grad,
        values_grad,
        memory_grad,
        query_grad,
        output_grad,
        gate_first_grad,
        up_first_grad,
        down_first_grad,
        memory_in_grad,
        memory_out_grad,
        gate_second_grad,
        up_second_grad,
        down_second_grad,
        gains_grad,
    )


def solution(mesh):
    seq, tp = mesh.shape["seq"], mesh.shape["tp"]
    fine = Mesh(
        mesh.devices.reshape(seq // 8, 2, 2, 2, tp // 2, 2), ("ze", "zh", "zl", "y", "x", "c")
    )
    tokens = P(None, SEQ, None)
    both = P(None, SEQ, TP)
    weight = P(SEQ, TP)
    return jax.shard_map(
        shards,
        mesh=fine,
        in_specs=(tokens, both, both, both, tokens) + (weight,) * 10 + (P(), P(), P()),
        out_specs=(tokens, tokens, both, both, both) + (weight,) * 10 + (P(None, SEQ),),
        check_vma=False,
    )
```

```python
import jax
import jax.numpy as jnp
from jax import lax
from jax.experimental import pallas as pl
from jax.sharding import Mesh
from jax.sharding import PartitionSpec as P

HD = 128
EPS = 1e-05
FILL = -1e30
BF = jnp.bfloat16
F32 = jnp.float32
SEQ = ("ze", "zh", "zl", "y")
TP = ("x", "c")
GROUP = ("zh", "zl", "y")
UNIT = ("zl", "y", "x", "c")


def swap(value, axis):
    return lax.ppermute(value, axis, [(0, 1), (1, 0)])


def after(value, earlier):
    return lax.optimization_barrier((value, earlier))[0]


def held(value, *earlier):
    earlier = jax.tree.leaves(earlier)
    if not earlier:
        return value
    anywhere = pl.BlockSpec(memory_space=pl.ANY)

    def body(*refs):
        pass

    return pl.pallas_call(
        body,
        in_specs=[anywhere] * (1 + len(earlier)),
        out_specs=anywhere,
        out_shape=jax.ShapeDtypeStruct(value.shape, value.dtype),
        input_output_aliases={0: 0},
        cost_estimate=pl.CostEstimate(flops=0, bytes_accessed=0, transcendentals=0),
    )(value, *earlier)


def dot(a, b):
    return jnp.dot(a, b, preferred_element_type=F32)


def dot_nt(a, b):
    return lax.dot_general(a, b, (((1,), (1,)), ((), ())), preferred_element_type=F32)


def dot_tn(a, b):
    return lax.dot_general(a, b, (((0,), (0,)), ((), ())), preferred_element_type=F32)


def in_order(bit, own, other, axis):
    return jnp.where(
        bit == 0,
        jnp.concatenate([own, other], axis),
        jnp.concatenate([other, own], axis),
    )


def half(value, bit, axis):
    size = value.shape[axis] // 2
    return lax.dynamic_slice_in_dim(value, bit * size, size, axis)


def trade(value, axes):
    return lax.all_to_all(value, axes, split_axis=0, concat_axis=0, tiled=True)


def copies(value, n):
    return jnp.broadcast_to(value[None], (n,) + value.shape)


def over_ze(value):
    if lax.axis_size("ze") == 1:
        return value
    return lax.all_gather(value, "ze", axis=0, tiled=True)


def total_ze(value):
    if lax.axis_size("ze") == 1:
        return value
    return lax.psum_scatter(value.astype(BF), "ze", scatter_dimension=0, tiled=True).astype(F32)


def cut(w):
    r, k = w.shape[0], w.shape[1] // 4

    def body(w_ref, out_ref):
        out_ref[0] = w_ref[...]

    return pl.pallas_call(
        body,
        grid=(8,),
        in_specs=[pl.BlockSpec((r, k), lambda i: (0, i % 4))],
        out_specs=pl.BlockSpec((1, r, k), lambda i: (i, 0, 0)),
        out_shape=jax.ShapeDtypeStruct((8, r, k), w.dtype),
        cost_estimate=pl.CostEstimate(flops=0, bytes_accessed=24 * r * k, transcendentals=0),
    )(w)


def fold(t):
    r, k = t.shape[1:]

    def body(a_ref, b_ref, out_ref):
        out_ref[...] = a_ref[0].astype(F32) + b_ref[0].astype(F32)

    return pl.pallas_call(
        body,
        grid=(4,),
        in_specs=[
            pl.BlockSpec((1, r, k), lambda i: (i, 0, 0)),
            pl.BlockSpec((1, r, k), lambda i: (i + 4, 0, 0)),
        ],
        out_specs=pl.BlockSpec((r, k), lambda i: (0, i)),
        out_shape=jax.ShapeDtypeStruct((r, 4 * k), F32),
        cost_estimate=pl.CostEstimate(flops=0, bytes_accessed=32 * r * k, transcendentals=0),
    )(t, t)


class Place:
    def __init__(self, width):
        self.zh = lax.axis_index("zh")
        self.zl = lax.axis_index("zl")
        self.x = lax.axis_index("x")
        self.y = lax.axis_index("y")
        self.c = lax.axis_index("c")
        self.ze = lax.axis_size("ze")
        self.rows = width // (self.ze * 8)
        self.line = []
        self.first = []

    def ordered(self, value, axes):
        if self.line:
            value = after(value, self.line[-1])
        if self.first:
            value = after(value, tuple(self.first))
            self.first = []
        self.line.append(trade(value, axes))
        return self.line[-1]

    def gather(self, w):
        r, k = w.shape
        w = self.ordered(cut(w), GROUP)
        w = over_ze(w.reshape(8 * r, k // 4))
        own = lax.all_gather(w, "x", axis=1, tiled=True)
        return own, swap(own, "c")

    def open_grad(self, left, far):
        part = dot_tn(left, far).astype(BF)
        return part, swap(part, "c")

    def close_grad(self, left, own, got):
        part = (dot_tn(left, own) + got.astype(F32)).astype(BF)
        t = lax.psum_scatter(part, "x", scatter_dimension=1, tiled=True)
        t = total_ze(t).astype(BF).reshape(8, self.rows, -1)
        return part, fold(self.ordered(t, GROUP))

    def gather_rows(self, w, swapped=False):
        a = self.ordered(copies(w, 4), ("zh", "zl"))
        a = over_ze(a)
        if swapped:
            return in_order(self.y, a, swap(a, "y"), 1).reshape(-1, w.shape[1])
        return lax.all_gather(a, "y", axis=1, tiled=True).reshape(-1, w.shape[1])

    def scatter_rows(self, left, right, swapped=False):
        part = dot_tn(left, right).astype(BF)
        t = part.reshape(-1, 2 * self.rows, right.shape[1])
        if swapped:
            got = swap(half(t, 1 - self.y, 1), "y")
            t = half(t, self.y, 1).astype(F32) + got.astype(F32)
        else:
            t = lax.psum_scatter(t, "y", scatter_dimension=1, tiled=True)
        t = self.ordered(total_ze(t).astype(BF), ("zh", "zl")).astype(F32)
        return part, (t[0] + t[1]) + (t[2] + t[3])

    def spread(self, v):
        h = v.shape[1] // 2
        vy = swap(v, "y")
        vz = swap(v, "zl")
        both = jnp.concatenate([swap(vz[:, :h], "y"), swap(vy[:, h:], "zl")], 1)
        return jnp.concatenate([v, vy, vz, both], 0)

    def collect(self, part):
        t, d = part.shape
        h = d // 2
        part = part.reshape(4, t // 4, d)
        a, b = part[..., :h], part[..., h:]
        got_a = swap(a[2:].astype(BF), "zl").astype(F32)
        got_b = swap(b[1::2].astype(BF), "y").astype(F32)
        a_y = (a[1] + got_a[1]).astype(BF)
        b_z = (b[2] + got_b[1]).astype(BF)
        a0 = a[0] + got_a[0] + swap(a_y, "y").astype(F32)
        b0 = b[0] + got_b[0] + swap(b_z, "zl").astype(F32)
        return jnp.concatenate([a0, b0], 1)

    def own_rows(self, v):
        mb, t, d = v.shape
        v = v.reshape(mb, 4, t // 4, d)
        v = lax.dynamic_slice_in_dim(v, self.x * 2 + self.c, 1, 1)
        return v.reshape(mb * t // 4, d)

    def spread_tp(self, v, mb):
        d = v.shape[1]
        v = v.reshape(mb, 1, -1, d)
        pair = in_order(self.x, v, swap(v, "x"), 1)[:, :, None]
        full = in_order(self.c, pair, swap(pair, "c"), 2)
        return full.reshape(mb, -1, d)

    def collect_tp(self, part, mb):
        t, d = part.shape
        part = part.reshape(mb, 2, 2, t // (4 * mb), d)
        mine = half(part, self.c, 2)
        mine = mine + swap(half(part, 1 - self.c, 2).astype(BF), "c").astype(F32)
        own = half(mine, self.x, 1)
        own = own + swap(half(mine, 1 - self.x, 1).astype(BF), "x").astype(F32)
        return own.reshape(t // 4, d)

    def trade_half(self, v, bit, axis, name):
        return jnp.stack([half(v, bit, axis), swap(half(v, 1 - bit, axis), name)])

    def memory_in(self, m):
        mb, t, k = m.shape
        v = m.reshape(mb, 2, 2, t // 4, 2, 2, k // 4).transpose(4, 5, 1, 2, 0, 3, 6)
        v = self.trade_half(v, self.c, 3, "c")
        v = self.trade_half(v, self.x, 3, "x")
        v = jnp.where(self.x == 1, jnp.flip(v, 0), v)
        v = self.trade_half(v, self.y, 3, "y")
        v = self.trade_half(v, self.zl, 3, "zl")
        v = v.reshape(2, 2, 2, 2, mb * t // 4, k // 4)
        v = v.transpose(3, 0, 1, 4, 2, 5).reshape(2, mb * t, k // 2)
        return v[0], v[1]

    def memory_out(self, own, far, mb):
        t, k = own.shape[0], own.shape[1] * 2
        v = jnp.stack([own, far]).astype(BF).reshape(2, 2, 2, t // 4, 2, k // 4)
        v = v.transpose(0, 4, 1, 2, 3, 5)
        v = in_order(self.zl, v[:, :, :1], swap(v[:, :, 1:], "zl"), 2)
        v = in_order(self.y, v[:, :, :, :1], swap(v[:, :, :, 1:], "y"), 3)
        v = in_order(self.c, v[:1][None], swap(v[1:], "c")[None], 0)
        v = v[:, 0]
        v = in_order(self.x, half(v, self.x, 1)[None], swap(half(v, 1 - self.x, 1), "x")[None], 0)
        v = v.reshape(2, 2, 2, 2, mb, t // (4 * mb), k // 4)
        return v.transpose(4, 0, 1, 5, 2, 3, 6).reshape(mb, t // mb, k).astype(F32)


def rms(v, g):
    r = lax.rsqrt(jnp.mean(v * v, axis=-1, keepdims=True) + EPS)
    return v * r * g


def rms_back(v, g, dn):
    r = lax.rsqrt(jnp.mean(v * v, axis=-1, keepdims=True) + EPS)
    gain = jnp.sum(dn * v * r, axis=0)
    gd = g * dn
    return r * gd - v * (r * r * r) * jnp.mean(v * gd, axis=-1, keepdims=True), gain


def silu_parts(v):
    s = jax.nn.sigmoid(v)
    return v * s, s * (1.0 + v * (1.0 - s))


def exchange(v):
    here = lax.axis_index(GROUP)
    out = []
    for k in range(8):
        block = lax.dynamic_index_in_dim(v, here ^ k, 0, keepdims=False)
        out.append(block if k == 0 else lax.ppermute(block, GROUP, [(i, i ^ k) for i in range(8)]))
    return out


def to_pairs(v):
    n, mb, t, k = v.shape
    v = v.reshape(n, mb, t, k // HD, HD).transpose(1, 3, 0, 2, 4).reshape(-1, n, t, HD)
    return jnp.concatenate(exchange(v), 1)


def from_pairs(v, mb, t):
    n = v.shape[0]
    here = lax.axis_index(GROUP)
    v = v.reshape(n, 8, t, HD)
    got = [v[:, 0]]
    for k in range(1, 8):
        got.append(lax.ppermute(v[:, k], GROUP, [(i, i ^ k) for i in range(8)]))
    v = jnp.stack(got)
    v = jnp.stack([lax.dynamic_index_in_dim(v, here ^ k, 0, keepdims=False) for k in range(8)])
    return v.reshape(mb, -1, n, t, HD).transpose(2, 0, 3, 1, 4).reshape(n, mb, t, -1)


def positions(order, ids, group_len):
    slots = jnp.arange(order.shape[0], dtype=jnp.int32)
    group = jnp.sum(
        jnp.where((ids // group_len)[:, None] == slots[None, :], order[None, :], 0), axis=1
    )
    return group * group_len + ids % group_len


def shards(
    stream_in,
    cache_keys,
    cache_values,
    memory,
    cotangent,
    query_proj,
    output_proj,
    gate_first,
    up_first,
    down_first,
    memory_in,
    memory_out,
    gate_second,
    up_second,
    down_second,
    norm_gains,
    group_order,
    seq_lengths,
):
    mb, tok, width = stream_in.shape
    at = Place(width)
    scaling = HD ** (-0.5)
    groups = group_order.shape[0]
    tokens = tok * at.ze * 8
    group_len = tokens // groups

    gains = norm_gains
    stream = stream_in
    r0 = at.own_rows(stream).astype(F32)

    wq = at.gather_rows(query_proj)
    cache = to_pairs(jnp.stack([cache_keys, cache_values], 0))
    keys, values = over_ze(cache[0]), over_ze(cache[1])
    g1 = at.gather(gate_first)
    u1 = at.gather(up_first)
    wo = at.gather_rows(output_proj, True)
    n1 = rms(stream.astype(F32).reshape(mb * tok, width), gains[0]).astype(BF)
    q = to_pairs(dot(n1, wq).astype(BF).reshape(1, mb, tok, -1))[0]
    at.first = [q]
    d1 = at.gather(down_first)

    pair = lax.axis_index(("zh", "zl", "y"))
    heads = cache_keys.shape[2] // HD
    batch = pair // heads
    length = lax.dynamic_slice_in_dim(seq_lengths, batch, 1, 0)
    q_rows = q.shape[0]
    k_rows = keys.shape[0]
    rows = jnp.arange(k_rows, dtype=jnp.int32)
    ids = rows // q_rows * q_rows + (rows % q_rows // tok ^ pair) * tok + rows % tok
    k_pos = positions(group_order, ids, group_len)
    q_pos = lax.dynamic_slice_in_dim(k_pos, lax.axis_index("ze") * q_rows, q_rows, 0)
    allowed = (k_pos[None, :] <= q_pos[:, None]) & (k_pos < length)[None, :]
    s = jnp.where(allowed, dot_nt(q, keys) * scaling, FILL)
    top = jnp.max(s, axis=1, keepdims=True)
    e = jnp.exp(s - top)
    total = jnp.sum(e, axis=1, keepdims=True)
    o = dot(e.astype(BF), values) / total
    lse = top + jnp.log(total)
    attn = from_pairs(o.astype(BF)[None], mb, tok).reshape(mb * tok, -1)

    at.first = [attn]
    mi, mo = at.gather(memory_in), at.gather(memory_out)
    x1 = r0 + at.collect_tp(dot_nt(attn, wo), mb)
    at.first = [x1]
    g2 = at.gather(gate_second)

    def ffn(x, gain, wg, wu, wd, pins):
        n = held(at.spread(rms(x, gain).astype(BF)), pins)
        gate = [dot(n, w) for w in wg]
        up = [dot(n, w) for w in wu]
        hidden = [(jax.nn.silu(g) * u).astype(BF) for g, u in zip(gate, up)]
        out = at.collect(dot_nt(hidden[0], wd[0]) + dot_nt(hidden[1], wd[1]))
        return x + out, (n, gate, up, hidden)

    x2, kept1 = ffn(x1, gains[1], g1, u1, d1, ())
    at.first = [kept1[0]]
    u2 = at.gather(up_second)
    d2 = at.gather(down_second)

    x2 = held(x2, at.line[9])
    mem = at.memory_in(memory)
    n3 = at.spread(rms(x2, gains[2]).astype(BF))
    za = [dot(n3, w) for w in mi]
    gm = [(m.astype(F32) * jax.nn.silu(z)).astype(BF) for m, z in zip(mem, za)]
    x3 = x2 + at.collect(dot_nt(gm[0], mo[0]) + dot_nt(gm[1], mo[1]))

    x4, kept2 = ffn(x3, gains[3], g2, u2, d2, d2[0])
    stream_out = at.spread_tp(x4.astype(BF), mb)

    cot = at.own_rows(cotangent)
    yb = at.spread(cot)

    zline = at.line

    def ffn_back(y, kept, wg, wu, wd, pins):
        n, gate, up, hidden = kept
        far_d, got_d = at.open_grad(y, hidden[1])
        y2 = after(y, far_d)
        dg, du = [], []
        for g, u, w in zip(gate, up, wd):
            dh = dot(y2, w)
            act, slope = silu_parts(g)
            dg.append((dh * u * slope).astype(BF))
            du.append((dh * act).astype(BF))
        part_d, down_grad = at.close_grad(y, hidden[0], got_d)
        dg, du = after((dg, du), (part_d,) + pins)
        dn = dot_nt(dg[0], wg[0]) + dot_nt(dg[1], wg[1])
        dn = dn + dot_nt(du[0], wu[0]) + dot_nt(du[1], wu[1])
        far_g, got_g = at.open_grad(n, dg[1])
        far_u, got_u = at.open_grad(n, du[1])
        dn = after(at.collect(dn), (far_g, far_u))
        return dn, down_grad, (n, dg[0], got_g), (n, du[0], got_u)

    dn4, down_second_grad, open_g, open_u = ffn_back(yb, kept2, g2, u2, d2, ())
    back, gain4 = rms_back(x3, gains[3], dn4)
    dx3 = cot.astype(F32) + back

    part_g, gate_second_grad = at.close_grad(*open_g)
    yg = after(at.spread(dx3.astype(BF)), part_g)
    part_u, up_second_grad = at.close_grad(*open_u)
    far, got = at.open_grad(yg, gm[1])
    dz, dm = [], []
    for w, z, m in zip(mo, za, mem):
        dgm = dot(yg, w)
        act, slope = silu_parts(z)
        dm.append(dgm * act)
        dz.append((dgm * m.astype(F32) * slope).astype(BF))
    dz = after(dz, (part_u, far))
    dn3 = dot_nt(dz[0], mi[0]) + dot_nt(dz[1], mi[1])
    part_o, memory_out_grad = at.close_grad(yg, gm[0], got)
    far, got = at.open_grad(n3, dz[1])
    dn3 = after(at.collect(dn3), (part_o, far, zline[10]))
    memory_grad = at.memory_out(dm[0], dm[1], mb)
    back, gain3 = rms_back(x2, gains[2], dn3)
    dx2 = held(dx3 + back, zline[11])

    part_i, memory_in_grad = at.close_grad(n3, dz[0], got)
    ya = after(at.spread(dx2.astype(BF)), (part_i, zline[11]))
    dn2, down_first_grad, open_g, open_u = ffn_back(ya, kept1, g1, u1, d1, (zline[12],))
    dn2 = after(dn2, (zline[13], zline[14]))
    back, gain2 = rms_back(x1, gains[1], dn2)
    dx1 = held(dx2 + back, zline[15])

    part_g, gate_first_grad = at.close_grad(*open_g)
    yo = after(at.spread_tp(dx1.astype(BF), mb), (part_g, zline[15])).reshape(mb * tok, width)
    part_u, up_first_grad = at.close_grad(*open_u)
    do = to_pairs(dot(yo, wo).astype(BF).reshape(1, mb, tok, -1))[0]
    do = after(do, part_u)
    part_w, output_grad = at.scatter_rows(yo, attn)
    do = held(do, zline[16])
    delta = jnp.sum(do.astype(F32) * o, axis=1, keepdims=True)
    p = jnp.exp(s - lse)
    ds = (p * (dot_nt(do, values) - delta)).astype(BF)
    dq = after((dot(ds, keys) * scaling).astype(BF)[None], (part_w, zline[16]))
    dq = from_pairs(dq, mb, tok)
    dk = total_ze(dot_tn(ds, q) * scaling).astype(BF)
    dv = total_ze(dot_tn(p.astype(BF), do)).astype(BF)
    dkv = from_pairs(held(jnp.stack([dk, dv]), dq), mb, tok).astype(F32)
    keys_grad, values_grad = dkv[0], dkv[1]
    dq = dq.reshape(mb * tok, -1)
    dn1 = at.collect_tp(held(dot_nt(dq, wq), zline[17]), mb)
    _, query_grad = at.scatter_rows(n1, dq, True)
    back, gain1 = rms_back(r0, gains[0], dn1)
    stream_grad = at.spread_tp((dx1 + back).astype(BF), mb).astype(F32)

    gain = jnp.stack([gain1, gain2, gain3, gain4])
    for axis in ("c", "x", "y", "zh", "zl"):
        gain = gain + swap(gain, axis)
    if at.ze > 1:
        gain = lax.psum(gain, "ze")
    spot = lax.axis_index(SEQ)
    gains_grad = lax.dynamic_slice_in_dim(gain, spot * at.rows, at.rows, 1)

    return (
        stream_out,
        stream_grad,
        keys_grad,
        values_grad,
        memory_grad,
        query_grad,
        output_grad,
        gate_first_grad,
        up_first_grad,
        down_first_grad,
        memory_in_grad,
        memory_out_grad,
        gate_second_grad,
        up_second_grad,
        down_second_grad,
        gains_grad,
    )


def solution(mesh):
    seq, tp = mesh.shape["seq"], mesh.shape["tp"]
    fine = Mesh(
        mesh.devices.reshape(seq // 8, 2, 2, 2, tp // 2, 2), ("ze", "zh", "zl", "y", "x", "c")
    )
    tokens = P(None, SEQ, None)
    both = P(None, SEQ, TP)
    weight = P(SEQ, TP)
    return jax.shard_map(
        shards,
        mesh=fine,
        in_specs=(tokens, both, both, both, tokens) + (weight,) * 10 + (P(), P(), P()),
        out_specs=(tokens, tokens, both, both, both) + (weight,) * 10 + (P(None, SEQ),),
        check_vma=False,
    )
```
